128 devices in a mesh: slab: 8 (over x_lo, y), grp: 16 (over x_hi, z, core).
Axes of the slice: x: 4 (x_hi: 2, x_lo: 2; x = x_hi * 2 + x_lo), y: 4, z: 4, core: 2. Of those that a mesh axis runs over, the one named last changes fastest.
Arguments:
- cell_density: float32 [8, 32, 2, 8], P('slab', 'grp'), may hold values from 1 to 10
- cell_slot: int32 [8, 32, 2, 8], P('slab', 'grp'), may hold values from 0 to 7, each once within a row
- neighbours: int32 [8, 32, 2, 6], P('slab', 'grp'), may hold values from -1 to 511, as said below
- face_code: int32 [8, 32, 2, 6], P('slab', 'grp'), may hold values from 0 to 15, as said below
- stiffness: float32 [64, 64], replicated, as said below
- prolong: float32 [8, 64, 64], replicated, as said below
- penalty: float32 [16, 64, 64], replicated, as said below
- fine_rhs: bfloat16 [8, 32, 2, 8, 4096], P('slab', 'grp'), may hold values from -24 to 24
Outputs:
- coarse_correction: float32 [8, 32, 2, 4096], P(None, 'grp')
The draws below stay inside these ranges and needn't reach their ends.
Inputs may be any that keep to these rules, and one draw needn't show every extreme that they name: `neighbours`: aggregates form a lattice of 8 x 32 x 2; faces in the order -first, +first, -second, +second, -third, +third dimension. Each entry is the number of the lattice neighbour across that face, or -1 where the face lies on the lattice boundary or is a wall; a wall seen from one side is a wall from the other. `face_code`: equal on both sides of every face that is not -1 in neighbours. `cell_slot`: the 8 cells of each aggregate hold each slot once. `stiffness`: Symmetric, each diagonal entry larger than the sum of the magnitudes of the other entries of its row. `prolong`: each diagonal entry larger than the sum of the magnitudes of the other entries of its row. `penalty`: Symmetric, each diagonal entry larger than the sum of the magnitudes of the other entries of its row.
All inputs are finite; a program needn't handle non-finite values.
Results may differ from the reference program's by a relative error of at most 0.0003.
Values sent between devices are 32-bit elements; how exact they have to be, the bound alone decides.
A program may use at most 128 MiB of HBM per device.

```python
import math
import jax
import jax.numpy as jnp
from jax import lax

DOF = 64
NRHS = 64
KIDS = 8
NCODE = 16
SWEEPS = 8
LC = 2
AX = 8
BX = 32


def lattice_faces(key):
    walls = jax.random.randint(jax.random.fold_in(key, 11), (3, AX, BX, LC), 0, 4) == 0
    pattern = jax.random.randint(jax.random.fold_in(key, 12), (AX, BX, LC), 0, NCODE)
    first_idx = lax_iota(0)
    second_idx = lax_iota(1)
    third_idx = lax_iota(2)
    flat = (first_idx * BX + second_idx) * LC + third_idx
    sizes_all = (AX, BX, LC)
    strides = (BX * LC, LC, 1)
    places = (first_idx, second_idx, third_idx)
    links = []
    codes = []
    for axis in range(3):
        down_open = (places[axis] > 0) & jnp.logical_not(jnp.roll(walls[axis], 1, axis=axis))
        up_open = (places[axis] + 1 < sizes_all[axis]) & jnp.logical_not(walls[axis])
        links.append(jnp.where(down_open, flat - strides[axis], -1))
        links.append(jnp.where(up_open, flat + strides[axis], -1))
        codes.append((pattern + jnp.roll(pattern, 1, axis=axis)) % NCODE)
        codes.append((pattern + jnp.roll(pattern, -1, axis=axis)) % NCODE)
    return (jnp.stack(links, axis=-1).astype(jnp.int32), jnp.stack(codes, axis=-1).astype(jnp.int32))


def lax_iota(axis):
    shape = (AX, BX, LC)
    return jax.lax.broadcasted_iota(jnp.int32, shape, axis)


def draw_neighbours(key, part):
    return lattice_faces(key)[0]


def draw_face_code(key, part):
    return lattice_faces(key)[1]


def dominant(key, lead, size, bound, base, spread, symmetric):
    raw = jax.random.uniform(jax.random.fold_in(key, 21), lead + (size, size), jnp.float32, -bound, bound)
    if symmetric:
        raw = 0.5 * (raw + jnp.swapaxes(raw, -1, -2))
    eye = jnp.eye(size, dtype=jnp.float32)
    centre = base + jax.random.uniform(jax.random.fold_in(key, 22), lead + (size, 1), jnp.float32, 0.0, spread)
    return raw * (1.0 - eye) + eye * centre


def draw_stiffness(key, part):
    return dominant(key, (), DOF, 1.8 / DOF, 3.0, 1.0, True)


def draw_prolong(key, part):
    return dominant(key, (KIDS,), DOF, 0.9 / DOF, 1.0, 0.5, False)


def draw_penalty(key, part):
    return dominant(key, (NCODE,), DOF, 1.8 / DOF, 3.0, 2.0, True)


def block_scale(stream_key, shape, shards, low, high):
    level, own = 1.0, jax.random.fold_in(stream_key, 6)
    for axis_at, shards_of in shards:
        heights = jnp.exp(jax.random.uniform(jax.random.fold_in(own, axis_at), (shards_of,), jnp.float32, low / len(shards), high / len(shards)))
        level = level * jnp.repeat(heights, shape[axis_at] // shards_of).reshape([-1 if axis == axis_at else 1 for axis in range(len(shape))])
    return level


def centred(rng, dims, scale, reach, cuts=(), held_as=jnp.bfloat16):
    array = jax.random.normal(rng, dims, jnp.float32) * scale
    if len(cuts) > 0:
        array = block_scale(rng, dims, cuts, -0.22, 0.18) * array
    return jnp.clip(array, min=-reach, max=reach).astype(held_as)


def setup_inputs(seed: int = 0) -> dict:
    streams_of = jax.random.split(jax.random.key(seed), 9)
    cell_density = jnp.clip(jnp.exp(math.log(10.0) - 2.3025851 * jax.random.uniform(streams_of[0], (AX, BX, LC, KIDS), jnp.float32) ** block_scale(streams_of[0], (AX, BX, LC, KIDS), ((0, 8), (1, 16)), -0.2, 0.2)), 1.0, 10.0)
    cell_slot = jax.vmap(lambda own: jax.random.permutation(own, KIDS))(jax.random.split(streams_of[1], AX * BX * LC)).reshape((AX, BX, LC, KIDS)).astype(jnp.int32)
    neighbours = draw_neighbours(jax.random.fold_in(streams_of[8], 71), 0)
    face_code = draw_face_code(jax.random.fold_in(streams_of[8], 71), 0)
    stiffness = draw_stiffness(jax.random.fold_in(streams_of[8], 71), 0)
    prolong = draw_prolong(jax.random.fold_in(streams_of[8], 71), 0)
    penalty = draw_penalty(jax.random.fold_in(streams_of[8], 71), 0)
    fine_rhs = centred(streams_of[7], (AX, BX, LC, KIDS, DOF * NRHS), 4.0, 24.0, ((0, 8), (1, 16)))
    return {"cell_density": cell_density, "cell_slot": cell_slot, "neighbours": neighbours, "face_code": face_code, "stiffness": stiffness, "prolong": prolong, "penalty": penalty, "fine_rhs": fine_rhs}


def reference(cell_density, cell_slot, neighbours, face_code, stiffness, prolong, penalty, fine_rhs):
    highest = lax.Precision.HIGHEST
    count = AX * BX * LC
    templates = jnp.einsum('sji,jk,skl->sil', prolong, stiffness, prolong, precision=highest)
    density = cell_density.reshape(count, KIDS)
    slots = cell_slot.reshape(count, KIDS)
    links = neighbours.reshape(count, 6)
    codes = face_code.reshape(count, 6)
    mean_rho = jnp.mean(density, axis=1)
    onehot = (slots[:, :, None] == jnp.arange(KIDS, dtype=jnp.int32)[None, None, :]).astype(jnp.float32)
    weights = jnp.einsum('aq,aqs->as', 1.0 / density, onehot, precision=highest)
    present = links >= 0
    safe_links = jnp.where(present, links, 0).astype(jnp.int32)
    others = mean_rho[safe_links]
    face_weight = jnp.where(present, 2.0 / (mean_rho[:, None] + others), jnp.float32(0.0))
    code_hot = (codes[:, :, None] == jnp.arange(NCODE, dtype=jnp.int32)[None, None, :]).astype(jnp.float32) * face_weight[:, :, None]
    flat_templ = templates.reshape(KIDS, DOF * DOF)
    flat_pen = penalty.reshape(NCODE, DOF * DOF)
    cell_part = jnp.dot(weights, flat_templ, precision=highest)
    face_part = jnp.dot(jnp.sum(code_hot, axis=1), flat_pen, precision=highest)
    diag_blocks = (cell_part + face_part).reshape(count, DOF, DOF)
    off_blocks = (-jnp.dot(code_hot.reshape(count * 6, NCODE), flat_pen, precision=highest)).reshape(count, 6, DOF, DOF)
    cell_prolong = prolong[slots]
    cell_rhs = fine_rhs.reshape(count, KIDS, DOF, NRHS).astype(jnp.float32)
    coarse_rhs = jnp.einsum('aqji,aqjr->air', cell_prolong, cell_rhs, precision=highest)
    jacobi = jnp.diagonal(diag_blocks, axis1=1, axis2=2)
    totals = jnp.sum(jnp.abs(diag_blocks), axis=2) + jnp.sum(jnp.abs(off_blocks), axis=(1, 3))
    upper = jnp.max(totals / jacobi)
    jacobi = jacobi[:, :, None]
    gather_index = jnp.where(present, links, count).astype(jnp.int32)

    def apply_op(vector):
        result = jnp.einsum('aij,ajr->air', diag_blocks, vector, precision=highest)
        padded = jnp.concatenate([vector, jnp.zeros((1, DOF, NRHS), jnp.float32)], axis=0)
        for face in range(6):
            result = result + jnp.einsum('aij,ajr->air', off_blocks[:, face], padded[gather_index[:, face]], precision=highest)
        return result

    lower = upper / 10.0
    centre_val = 0.5 * (upper + lower)
    half_width = 0.5 * (upper - lower)
    sigma_val = centre_val / half_width
    damping = 1.0 / sigma_val
    resid = coarse_rhs
    update = resid / jacobi / centre_val
    solution = update
    for sweep in range(SWEEPS):
        resid = resid - apply_op(update)
        damping_next = 1.0 / (2.0 * sigma_val - damping)
        update = damping_next * damping * update + (2.0 * damping_next / half_width) * (resid / jacobi)
        solution = solution + update
        damping = damping_next
    return solution.reshape(AX, BX, LC, DOF * NRHS)
```

```python
import functools

import jax
import jax.numpy as jnp
from jax import lax
from jax.experimental import pallas as pl
from jax.experimental.pallas import tpu as pltpu
from jax.sharding import PartitionSpec as P

SWEEPS = 8

MESH = pl.DeviceIdType.MESH
f32, bf16 = jnp.float32, jnp.bfloat16
highest = lax.Precision.HIGHEST
DOWN_A, UP_A, DOWN_B, UP_B, DOWN_C, UP_C = range(6)


def split(x):
    hi = x.astype(bf16)
    return hi, (x - hi.astype(f32)).astype(bf16)


def mm(a, b, precision=None):
    return lax.dot_general(
        a, b, (((1,), (0,)), ((), ())), precision=precision, preferred_element_type=f32
    )


def swap_halves(x):
    return pltpu.roll(x, x.shape[-1] // 2, x.ndim - 1)


def kernel(
    slabs,
    grps,
    dens,
    slots,
    neigh,
    codes,
    stiff,
    prolong,
    penalty,
    fine,
    out,
    rho,
    rho_in,
    templ,
    wide,
    own_op,
    far_op,
    rhs,
    resid,
    ijac,
    total,
    w0,
    send,
    from_a,
    from_b,
    top_b,
    top_a,
    final,
    rho_ss,
    rho_rs,
    halo_ss,
    halo_rs,
    topb_ss,
    topb_rs,
    topa_ss,
    topa_rs,
    out_ss,
    out_rs,
    local_sem,
):
    a = lax.axis_index("slab")
    b = lax.axis_index("grp")
    up_a, down_a = lax.rem(a + 1, slabs), lax.rem(a + slabs - 1, slabs)
    up_b, down_b = lax.rem(b + 1, grps), lax.rem(b + grps - 1, grps)

    barrier = pltpu.get_barrier_semaphore()

    def greet_b(d, _):
        pl.semaphore_signal(
            barrier, inc=1, device_id=(a, lax.rem(b + d, grps)), device_id_type=MESH
        )
        return 0

    def greet_a(d, _):
        pl.semaphore_signal(
            barrier, inc=1, device_id=(lax.rem(a + d, slabs), b), device_id_type=MESH
        )
        return 0

    lax.fori_loop(1, grps, greet_b, 0)
    lax.fori_loop(1, slabs, greet_a, 0)

    left = lax.broadcasted_iota(jnp.int32, (64, 128), 1) < 64

    for l in range(4):
        mean = dens[0, l // 2, l % 2, 0]
        for c in range(1, 8):
            mean = mean + dens[0, l // 2, l % 2, c]
        rho[l : l + 1, :] = jnp.full((1, 128), mean * 0.125, f32)
    rho[4:8, :] = jnp.ones((4, 128), f32)

    pl.semaphore_wait(barrier, grps - 1 + slabs - 1)

    def rho_copy(i, to_a, to_b):
        return pltpu.make_async_remote_copy(
            src_ref=rho,
            dst_ref=rho_in.at[i],
            send_sem=rho_ss.at[i],
            recv_sem=rho_rs.at[i],
            device_id=(to_a, to_b),
            device_id_type=MESH,
        )

    rho_copies = [
        rho_copy(DOWN_A, up_a, b),
        rho_copy(UP_A, down_a, b),
        rho_copy(DOWN_B, a, up_b),
        rho_copy(UP_B, a, down_b),
    ]
    for copy in rho_copies:
        copy.start()

    for s in range(8):
        p = prolong[s]
        kp = mm(stiff[...], p, highest)
        templ[s] = mm(p.T, kp, highest)

    for h in range(2):
        for s in range(8):
            wide[pl.ds(s * 32, 32), h * 64 : h * 64 + 64] = prolong[
                s, pl.ds(h, 32, stride=2), :
            ]
    w_hi, w_lo = split(wide[...].T)
    w_both = jnp.concatenate([w_hi, w_lo], axis=0)
    row = lax.broadcasted_iota(jnp.int32, (256, 256), 0)
    col = lax.broadcasted_iota(jnp.int32, (256, 256), 1)
    same_pair = lax.rem(row, 32) == col // 8
    lane = lax.rem(lax.broadcasted_iota(jnp.int32, (1, 256), 1), 8)
    parts = []
    for l in range(4):
        slot_of = jnp.zeros((1, 256), jnp.int32)
        for c in range(8):
            slot_of = jnp.where(lane == c, slots[0, l // 2, l % 2, c], slot_of)
        pick = jnp.where(same_pair & (row // 32 == slot_of), 1.0, 0.0).astype(bf16)
        ordered = mm(pick, fine[l]).astype(bf16)
        both = mm(w_both, ordered)
        parts.append(both[:128] + both[128:])
    for m in range(2):
        y0, y1 = parts[2 * m], parts[2 * m + 1]
        rhs[m] = jnp.where(left, y0[:64], y1[64:]) + swap_halves(
            jnp.where(left, y1[:64], y0[64:])
        )

    for copy in rho_copies:
        copy.wait()
    eye = lax.broadcasted_iota(jnp.int32, (64, 64), 0) == lax.broadcasted_iota(
        jnp.int32, (64, 64), 1
    )
    top = jnp.zeros((1, 1), f32)
    for m in range(2):
        jacs = []
        for k in range(2):
            l = 2 * m + k
            mine = rho[l : l + 1, :]
            faces = {
                DOWN_A: rho_in[DOWN_A, l : l + 1, :],
                UP_A: rho_in[UP_A, l : l + 1, :],
                DOWN_B: rho_in[DOWN_B, 2 + k : 3 + k, :] if m == 0 else rho[k : k + 1, :],
                UP_B: rho[2 + k : 3 + k, :] if m == 0 else rho_in[UP_B, k : k + 1, :],
                (UP_C if k == 0 else DOWN_C): rho[2 * m + 1 - k : 2 * m + 2 - k, :],
            }
            diag = jnp.zeros((64, 64), f32)
            for c in range(8):
                weight = 1.0 / jnp.full((1, 64), dens[0, m, k, c], f32)
                diag = diag + weight * templ[slots[0, m, k, c]]
            offs = {}
            extent = jnp.zeros((64, 64), f32)
            for face, other in faces.items():
                present = (neigh[0, m, k, face] >= 0).astype(f32)
                weight = (2.0 / (mine + other) * present)[:, :64]
                block = weight * penalty[codes[0, m, k, face]]
                diag = diag + block
                extent = extent + jnp.abs(block)
                offs[face] = -block
            jac = jnp.sum(jnp.where(eye, diag, 0.0), axis=1, keepdims=True)
            sums = jnp.sum(jnp.abs(diag) + extent, axis=1, keepdims=True)
            top = jnp.maximum(top, jnp.max(sums / jac, axis=0, keepdims=True))
            jacs.append(1.0 / jac)
            in_pair = UP_B if m == 0 else DOWN_B
            out_pair = DOWN_B if m == 0 else UP_B
            in_c = UP_C if k == 0 else DOWN_C
            for op, three in (
                (own_op, (diag, offs[in_pair], offs[in_c])),
                (far_op, (offs[DOWN_A], offs[UP_A], offs[out_pair])),
            ):
                for at, width, value in (
                    (0, 128, jnp.concatenate(three[:2], axis=1)),
                    (128, 64, three[2]),
                ):
                    hi, lo = split(value)
                    op[m, k * 64 : k * 64 + 64, at : at + width] = hi
                    op[m, 128 + k * 64 : 192 + k * 64, at : at + width] = lo
        ijac[m] = jnp.where(left, jacs[0], jacs[1])

    top_b[0] = jnp.broadcast_to(top, (8, 128))

    def topb_copy(d):
        return pltpu.make_async_remote_copy(
            src_ref=top_b.at[0],
            dst_ref=top_b.at[d],
            send_sem=topb_ss.at[d],
            recv_sem=topb_rs.at[d],
            device_id=(a, lax.rem(b + d, grps)),
            device_id_type=MESH,
        )

    def topa_copy(d):
        return pltpu.make_async_remote_copy(
            src_ref=top_a.at[0],
            dst_ref=top_a.at[d],
            send_sem=topa_ss.at[d],
            recv_sem=topa_rs.at[d],
            device_id=(lax.rem(a + d, slabs), b),
            device_id_type=MESH,
        )

    def each(count, act):
        def body(d, _):
            act(d)
            return 0

        lax.fori_loop(1, count, body, 0)

    def halo(p):
        def copy(i, src, dst, to_a, to_b):
            return pltpu.make_async_remote_copy(
                src_ref=src,
                dst_ref=dst,
                send_sem=halo_ss.at[p, i],
                recv_sem=halo_rs.at[p, i],
                device_id=(to_a, to_b),
                device_id_type=MESH,
            )

        return [
            copy(0, send.at[p], from_a.at[p, 0], up_a, b),
            copy(1, send.at[p], from_a.at[p, 1], down_a, b),
            copy(2, send.at[p, 1], from_b.at[p, 0], a, up_b),
            copy(3, send.at[p, 0], from_b.at[p, 1], a, down_b),
        ]

    def product(op, m, stack):
        hi, lo = split(stack)
        one = mm(op[m], hi)
        return one[:128] + one[128:] + mm(op[m, :128, :], lo)

    def apply(p, copies):
        u = [send[p, 0], send[p, 1]]
        near = [
            product(own_op, m, jnp.concatenate([u[m], u[1 - m], swap_halves(u[m])], axis=0))
            for m in range(2)
        ]
        for copy in copies:
            copy.wait()
        result = []
        for m in range(2):
            stack = jnp.concatenate(
                [from_a[p, 0, m], from_a[p, 1, m], from_b[p, m]], axis=0
            )
            both = near[m] + product(far_op, m, stack)
            result.append(jnp.where(left, both[:64], both[64:]))
        return result

    each(grps, lambda d: topb_copy(d).start())
    copies = halo(0)
    for m in range(2):
        send[0, m] = rhs[m] * ijac[m]
    for copy in copies:
        copy.start()
    first = apply(0, copies)
    each(grps, lambda d: topb_copy(d).wait())
    top_a[0] = jnp.max(top_b[...], axis=0)
    each(slabs, lambda d: topa_copy(d).start())
    copies = halo(1)
    for m in range(2):
        w0[m] = first[m]
        send[1, m] = first[m] * ijac[m]
    for copy in copies:
        copy.start()
    second = apply(1, copies)
    each(slabs, lambda d: topa_copy(d).wait())
    upper = jnp.max(top_a[...], axis=0)[0:1, :]

    lower = upper / 10.0
    centre_val = 0.5 * (upper + lower)
    half_width = 0.5 * (upper - lower)
    sigma = centre_val / half_width
    over_centre = 1.0 / centre_val
    damp0 = 1.0 / sigma
    damp1 = 1.0 / (2.0 * sigma - damp0)
    keep1, gain1 = damp1 * damp0, 2.0 * damp1 / half_width
    damp2 = 1.0 / (2.0 * sigma - damp1)
    keep2, gain2 = damp2 * damp1, 2.0 * damp2 / half_width
    for m in range(2):
        update0 = send[0, m] * over_centre
        resid1 = rhs[m] - w0[m] * over_centre
        update1 = keep1 * update0 + gain1 * (resid1 * ijac[m])
        applied = (keep1 * over_centre) * w0[m] + gain1 * (w0[m] - over_centre * second[m])
        resid2 = resid1 - applied
        update2 = keep2 * update1 + gain2 * (resid2 * ijac[m])
        resid[m] = resid2
        total[m] = update0 + update1 + update2
        send[0, m] = update2

    def sweep(i, damp):
        p = lax.rem(i, 2)
        copies = halo(p)
        for copy in copies:
            copy.start()
        applied = apply(p, copies)
        damp_next = 1.0 / (2.0 * sigma - damp)
        keep, gain = damp_next * damp, 2.0 * damp_next / half_width
        for m in range(2):
            now = resid[m] - applied[m]
            resid[m] = now
            update = keep * send[p, m] + gain * (now * ijac[m])
            total[m] = total[m] + update
            send[1 - p, m] = update
        return damp_next

    lax.fori_loop(0, SWEEPS - 2, sweep, damp2)

    even = lax.rem(lax.broadcasted_iota(jnp.int32, (64, 128), 0), 2) == 0
    for m in range(2):
        x = total[m]
        turned = swap_halves(x)
        moved = jnp.where(even, pltpu.roll(turned, 63, 0), pltpu.roll(turned, 1, 0))
        final[m] = jnp.where(even == left, x, moved)

    def out_copy(d):
        return pltpu.make_async_remote_copy(
            src_ref=final,
            dst_ref=out.at[a],
            send_sem=out_ss.at[d],
            recv_sem=out_rs.at[d],
            device_id=(lax.rem(a + d, slabs), b),
            device_id_type=MESH,
        )

    each(slabs, lambda d: out_copy(d).start())
    keep_own = pltpu.make_async_copy(final, out.at[a], local_sem)
    keep_own.start()
    keep_own.wait()
    each(slabs, lambda d: out_copy(d).wait())


def local(slabs, grps, dens, slots, neigh, codes, stiff, prolong, penalty, fine):
    x = fine.reshape(4, 8, 32, 128).transpose(0, 2, 1, 3).reshape(4, 256, 128)
    smem = pl.BlockSpec(memory_space=pltpu.SMEM)
    vmem = pl.BlockSpec(memory_space=pltpu.VMEM)
    dma = pltpu.SemaphoreType.DMA
    result = pl.pallas_call(
        functools.partial(kernel, slabs, grps),
        out_shape=jax.ShapeDtypeStruct((slabs, 2, 64, 128), f32),
        in_specs=[smem] * 4 + [vmem] * 4,
        out_specs=pl.BlockSpec(memory_space=pl.ANY),
        scratch_shapes=[
            pltpu.VMEM((8, 128), f32),
            pltpu.VMEM((4, 8, 128), f32),
            pltpu.VMEM((8, 64, 64), f32),
            pltpu.VMEM((256, 128), f32),
            pltpu.VMEM((2, 256, 192), bf16),
            pltpu.VMEM((2, 256, 192), bf16),
            pltpu.VMEM((2, 64, 128), f32),
            pltpu.VMEM((2, 64, 128), f32),
            pltpu.VMEM((2, 64, 128), f32),
            pltpu.VMEM((2, 64, 128), f32),
            pltpu.VMEM((2, 64, 128), f32),
            pltpu.VMEM((2, 2, 64, 128), f32),
            pltpu.VMEM((2, 2, 2, 64, 128), f32),
            pltpu.VMEM((2, 2, 64, 128), f32),
            pltpu.VMEM((grps, 8, 128), f32),
            pltpu.VMEM((slabs, 8, 128), f32),
            pltpu.VMEM((2, 64, 128), f32),
            dma((4,)),
            dma((4,)),
            dma((2, 4)),
            dma((2, 4)),
            dma((grps,)),
            dma((grps,)),
            dma((slabs,)),
            dma((slabs,)),
            dma((slabs,)),
            dma((slabs,)),
            dma,
        ],
        compiler_params=pltpu.CompilerParams(
            collective_id=0, has_side_effects=True, vmem_limit_bytes=32 * 2**20
        ),
    )(dens, slots, neigh, codes, stiff, prolong, penalty, x)
    spread = result.reshape(slabs, 2, 32, 2, 128).transpose(0, 1, 3, 2, 4)
    return spread.reshape(slabs, 2, 2, 4096)


def solution(mesh):
    return jax.shard_map(
        functools.partial(local, mesh.shape["slab"], mesh.shape["grp"]),
        mesh=mesh,
        in_specs=(
            P("slab", "grp", None, None),
            P("slab", "grp", None, None),
            P("slab", "grp", None, None),
            P("slab", "grp", None, None),
            P(),
            P(),
            P(),
            P("slab", "grp", None, None, None),
        ),
        out_specs=P(None, "grp", None, None),
        check_vma=False,
    )
```

```python
import functools

import jax
import jax.numpy as jnp
from jax import lax
from jax.experimental import pallas as pl
from jax.experimental.pallas import tpu as pltpu
from jax.sharding import PartitionSpec as P

SWEEPS = 8

MESH = pl.DeviceIdType.MESH
f32, bf16 = jnp.float32, jnp.bfloat16
highest = lax.Precision.HIGHEST
DOWN_A, UP_A, DOWN_B, UP_B, DOWN_C, UP_C = range(6)


def split(x):
    hi = x.astype(bf16)
    return hi, (x - hi.astype(f32)).astype(bf16)


def mm(a, b, precision=None):
    return lax.dot_general(
        a, b, (((1,), (0,)), ((), ())), precision=precision, preferred_element_type=f32
    )


def swap_halves(x):
    return pltpu.roll(x, x.shape[-1] // 2, x.ndim - 1)


def kernel(
    slabs,
    grps,
    dens_hbm,
    slots_hbm,
    neigh_hbm,
    codes_hbm,
    stiff_hbm,
    prolong_hbm,
    penalty_hbm,
    fine_hbm,
    out,
    dens,
    slots,
    neigh,
    codes,
    stiff,
    prolong,
    penalty,
    fine,
    in_sems,
    rho,
    rho_in,
    templ,
    wide,
    own_op,
    far_op,
    rhs,
    resid,
    ijac,
    total,
    w0,
    send,
    from_a,
    from_b,
    top_b,
    top_a,
    final,
    rho_ss,
    rho_rs,
    halo_ss,
    halo_rs,
    topb_ss,
    topb_rs,
    topa_ss,
    topa_rs,
    out_ss,
    out_rs,
    local_sem,
):
    a = lax.axis_index("slab")
    b = lax.axis_index("grp")
    up_a, down_a = lax.rem(a + 1, slabs), lax.rem(a + slabs - 1, slabs)
    up_b, down_b = lax.rem(b + 1, grps), lax.rem(b + grps - 1, grps)

    dens_in, slots_in, neigh_in, codes_in, stiff_in, prolong_in, penalty_in, fine_in = loads = [
        pltpu.make_async_copy(src, dst, in_sems.at[i])
        for i, (src, dst) in enumerate(
            (
                (dens_hbm, dens),
                (slots_hbm, slots),
                (neigh_hbm, neigh),
                (codes_hbm, codes),
                (stiff_hbm, stiff),
                (prolong_hbm, prolong),
                (penalty_hbm, penalty),
                (fine_hbm, fine),
            )
        )
    ]
    for load in loads:
        load.start()

    barrier = pltpu.get_barrier_semaphore()

    def greet_b(d, _):
        pl.semaphore_signal(
            barrier, inc=1, device_id=(a, lax.rem(b + d, grps)), device_id_type=MESH
        )
        return 0

    def greet_a(d, _):
        pl.semaphore_signal(
            barrier, inc=1, device_id=(lax.rem(a + d, slabs), b), device_id_type=MESH
        )
        return 0

    lax.fori_loop(1, grps, greet_b, 0)
    lax.fori_loop(1, slabs, greet_a, 0)

    left = lax.broadcasted_iota(jnp.int32, (64, 128), 1) < 64

    dens_in.wait()
    for l in range(4):
        mean = dens[0, l // 2, l % 2, 0]
        for c in range(1, 8):
            mean = mean + dens[0, l // 2, l % 2, c]
        rho[l : l + 1, :] = jnp.full((1, 128), mean * 0.125, f32)
    rho[4:8, :] = jnp.ones((4, 128), f32)

    pl.semaphore_wait(barrier, grps - 1 + slabs - 1)

    def rho_copy(i, to_a, to_b):
        return pltpu.make_async_remote_copy(
            src_ref=rho,
            dst_ref=rho_in.at[i],
            send_sem=rho_ss.at[i],
            recv_sem=rho_rs.at[i],
            device_id=(to_a, to_b),
            device_id_type=MESH,
        )

    rho_copies = [
        rho_copy(DOWN_A, up_a, b),
        rho_copy(UP_A, down_a, b),
        rho_copy(DOWN_B, a, up_b),
        rho_copy(UP_B, a, down_b),
    ]
    for copy in rho_copies:
        copy.start()

    stiff_in.wait()
    prolong_in.wait()
    for s in range(8):
        p = prolong[s]
        kp = mm(stiff[...], p, highest)
        templ[s] = mm(p.T, kp, highest)

    for h in range(2):
        for s in range(8):
            wide[pl.ds(s * 32, 32), h * 64 : h * 64 + 64] = prolong[
                s, pl.ds(h, 32, stride=2), :
            ]
    w_hi, w_lo = split(wide[...].T)
    w_both = jnp.concatenate([w_hi, w_lo], axis=0)
    row = lax.broadcasted_iota(jnp.int32, (256, 256), 0)
    col = lax.broadcasted_iota(jnp.int32, (256, 256), 1)
    same_pair = lax.rem(row, 32) == col // 8
    lane = lax.rem(lax.broadcasted_iota(jnp.int32, (1, 256), 1), 8)
    parts = []
    slots_in.wait()
    fine_in.wait()
    for l in range(4):
        slot_of = jnp.zeros((1, 256), jnp.int32)
        for c in range(8):
            slot_of = jnp.where(lane == c, slots[0, l // 2, l % 2, c], slot_of)
        pick = jnp.where(same_pair & (row // 32 == slot_of), 1.0, 0.0).astype(bf16)
        ordered = mm(pick, fine[l]).astype(bf16)
        both = mm(w_both, ordered)
        parts.append(both[:128] + both[128:])
    for m in range(2):
        y0, y1 = parts[2 * m], parts[2 * m + 1]
        rhs[m] = jnp.where(left, y0[:64], y1[64:]) + swap_halves(
            jnp.where(left, y1[:64], y0[64:])
        )

    neigh_in.wait()
    codes_in.wait()
    penalty_in.wait()
    for copy in rho_copies:
        copy.wait()
    eye = lax.broadcasted_iota(jnp.int32, (64, 64), 0) == lax.broadcasted_iota(
        jnp.int32, (64, 64), 1
    )
    top = jnp.zeros((1, 1), f32)
    for m in range(2):
        jacs = []
        for k in range(2):
            l = 2 * m + k
            mine = rho[l : l + 1, :]
            faces = {
                DOWN_A: rho_in[DOWN_A, l : l + 1, :],
                UP_A: rho_in[UP_A, l : l + 1, :],
                DOWN_B: rho_in[DOWN_B, 2 + k : 3 + k, :] if m == 0 else rho[k : k + 1, :],
                UP_B: rho[2 + k : 3 + k, :] if m == 0 else rho_in[UP_B, k : k + 1, :],
                (UP_C if k == 0 else DOWN_C): rho[2 * m + 1 - k : 2 * m + 2 - k, :],
            }
            diag = jnp.zeros((64, 64), f32)
            for c in range(8):
                weight = 1.0 / jnp.full((1, 64), dens[0, m, k, c], f32)
                diag = diag + weight * templ[slots[0, m, k, c]]
            offs = {}
            extent = jnp.zeros((64, 64), f32)
            for face, other in faces.items():
                present = (neigh[0, m, k, face] >= 0).astype(f32)
                weight = (2.0 / (mine + other) * present)[:, :64]
                block = weight * penalty[codes[0, m, k, face]]
                diag = diag + block
                extent = extent + jnp.abs(block)
                offs[face] = -block
            jac = jnp.sum(jnp.where(eye, diag, 0.0), axis=1, keepdims=True)
            sums = jnp.sum(jnp.abs(diag) + extent, axis=1, keepdims=True)
            top = jnp.maximum(top, jnp.max(sums / jac, axis=0, keepdims=True))
            jacs.append(1.0 / jac)
            in_pair = UP_B if m == 0 else DOWN_B
            out_pair = DOWN_B if m == 0 else UP_B
            in_c = UP_C if k == 0 else DOWN_C
            for op, three in (
                (own_op, (diag, offs[in_pair], offs[in_c])),
                (far_op, (offs[DOWN_A], offs[UP_A], offs[out_pair])),
            ):
                for at, width, value in (
                    (0, 128, jnp.concatenate(three[:2], axis=1)),
                    (128, 64, three[2]),
                ):
                    hi, lo = split(value)
                    op[m, k * 64 : k * 64 + 64, at : at + width] = hi
                    op[m, 128 + k * 64 : 192 + k * 64, at : at + width] = lo
        ijac[m] = jnp.where(left, jacs[0], jacs[1])

    top_b[0] = jnp.broadcast_to(top, (8, 128))

    def topb_copy(d):
        return pltpu.make_async_remote_copy(
            src_ref=top_b.at[0],
            dst_ref=top_b.at[d],
            send_sem=topb_ss.at[d],
            recv_sem=topb_rs.at[d],
            device_id=(a, lax.rem(b + d, grps)),
            device_id_type=MESH,
        )

    def topa_copy(d):
        return pltpu.make_async_remote_copy(
            src_ref=top_a.at[0],
            dst_ref=top_a.at[d],
            send_sem=topa_ss.at[d],
            recv_sem=topa_rs.at[d],
            device_id=(lax.rem(a + d, slabs), b),
            device_id_type=MESH,
        )

    def each(count, act):
        def body(d, _):
            act(d)
            return 0

        lax.fori_loop(1, count, body, 0)

    def halo(p):
        def copy(i, src, dst, to_a, to_b):
            return pltpu.make_async_remote_copy(
                src_ref=src,
                dst_ref=dst,
                send_sem=halo_ss.at[p, i],
                recv_sem=halo_rs.at[p, i],
                device_id=(to_a, to_b),
                device_id_type=MESH,
            )

        return [
            copy(0, send.at[p], from_a.at[p, 0], up_a, b),
            copy(1, send.at[p], from_a.at[p, 1], down_a, b),
            copy(2, send.at[p, 1], from_b.at[p, 0], a, up_b),
            copy(3, send.at[p, 0], from_b.at[p, 1], a, down_b),
        ]

    def product(op, m, stack):
        hi, lo = split(stack)
        one = mm(op[m], hi)
        return one[:128] + one[128:] + mm(op[m, :128, :], lo)

    def apply(p, copies):
        u = [send[p, 0], send[p, 1]]
        near = [
            product(own_op, m, jnp.concatenate([u[m], u[1 - m], swap_halves(u[m])], axis=0))
            for m in range(2)
        ]
        for copy in copies:
            copy.wait()
        result = []
        for m in range(2):
            stack = jnp.concatenate(
                [from_a[p, 0, m], from_a[p, 1, m], from_b[p, m]], axis=0
            )
            both = near[m] + product(far_op, m, stack)
            result.append(jnp.where(left, both[:64], both[64:]))
        return result

    each(grps, lambda d: topb_copy(d).start())
    copies = halo(0)
    for m in range(2):
        send[0, m] = rhs[m] * ijac[m]
    for copy in copies:
        copy.start()
    first = apply(0, copies)
    each(grps, lambda d: topb_copy(d).wait())
    top_a[0] = jnp.max(top_b[...], axis=0)
    each(slabs, lambda d: topa_copy(d).start())
    copies = halo(1)
    for m in range(2):
        w0[m] = first[m]
        send[1, m] = first[m] * ijac[m]
    for copy in copies:
        copy.start()
    second = apply(1, copies)
    each(slabs, lambda d: topa_copy(d).wait())
    upper = jnp.max(top_a[...], axis=0)[0:1, :]

    lower = upper / 10.0
    centre_val = 0.5 * (upper + lower)
    half_width = 0.5 * (upper - lower)
    sigma = centre_val / half_width
    over_centre = 1.0 / centre_val
    damp0 = 1.0 / sigma
    damp1 = 1.0 / (2.0 * sigma - damp0)
    keep1, gain1 = damp1 * damp0, 2.0 * damp1 / half_width
    damp2 = 1.0 / (2.0 * sigma - damp1)
    keep2, gain2 = damp2 * damp1, 2.0 * damp2 / half_width
    for m in range(2):
        update0 = send[0, m] * over_centre
        resid1 = rhs[m] - w0[m] * over_centre
        update1 = keep1 * update0 + gain1 * (resid1 * ijac[m])
        applied = (keep1 * over_centre) * w0[m] + gain1 * (w0[m] - over_centre * second[m])
        resid2 = resid1 - applied
        update2 = keep2 * update1 + gain2 * (resid2 * ijac[m])
        resid[m] = resid2
        total[m] = update0 + update1 + update2
        send[0, m] = update2

    def sweep(i, damp):
        p = lax.rem(i, 2)
        copies = halo(p)
        for copy in copies:
            copy.start()
        applied = apply(p, copies)
        damp_next = 1.0 / (2.0 * sigma - damp)
        keep, gain = damp_next * damp, 2.0 * damp_next / half_width
        for m in range(2):
            now = resid[m] - applied[m]
            resid[m] = now
            update = keep * send[p, m] + gain * (now * ijac[m])
            total[m] = total[m] + update
            send[1 - p, m] = update
        return damp_next

    lax.fori_loop(0, SWEEPS - 2, sweep, damp2)

    even = lax.rem(lax.broadcasted_iota(jnp.int32, (64, 128), 0), 2) == 0
    for m in range(2):
        x = total[m]
        turned = swap_halves(x)
        moved = jnp.where(even, pltpu.roll(turned, 63, 0), pltpu.roll(turned, 1, 0))
        final[m] = jnp.where(even == left, x, moved)

    def out_copy(d):
        return pltpu.make_async_remote_copy(
            src_ref=final,
            dst_ref=out.at[a],
            send_sem=out_ss.at[d],
            recv_sem=out_rs.at[d],
            device_id=(lax.rem(a + d, slabs), b),
            device_id_type=MESH,
        )

    each(slabs, lambda d: out_copy(d).start())
    keep_own = pltpu.make_async_copy(final, out.at[a], local_sem)
    keep_own.start()
    keep_own.wait()
    each(slabs, lambda d: out_copy(d).wait())


def local(slabs, grps, dens, slots, neigh, codes, stiff, prolong, penalty, fine):
    x = fine.reshape(4, 8, 32, 128).transpose(0, 2, 1, 3).reshape(4, 256, 128)
    smem, vmem = pltpu.SMEM, pltpu.VMEM
    args = (dens, slots, neigh, codes, stiff, prolong, penalty, x)
    dma = pltpu.SemaphoreType.DMA
    result = pl.pallas_call(
        functools.partial(kernel, slabs, grps),
        out_shape=jax.ShapeDtypeStruct((slabs, 2, 64, 128), f32),
        in_specs=[pl.BlockSpec(memory_space=pl.ANY)] * 8,
        out_specs=pl.BlockSpec(memory_space=pl.ANY),
        scratch_shapes=[
            *(space(v.shape, v.dtype) for space, v in zip([smem] * 4 + [vmem] * 4, args)),
            dma((8,)),
            pltpu.VMEM((8, 128), f32),
            pltpu.VMEM((4, 8, 128), f32),
            pltpu.VMEM((8, 64, 64), f32),
            pltpu.VMEM((256, 128), f32),
            pltpu.VMEM((2, 256, 192), bf16),
            pltpu.VMEM((2, 256, 192), bf16),
            pltpu.VMEM((2, 64, 128), f32),
            pltpu.VMEM((2, 64, 128), f32),
            pltpu.VMEM((2, 64, 128), f32),
            pltpu.VMEM((2, 64, 128), f32),
            pltpu.VMEM((2, 64, 128), f32),
            pltpu.VMEM((2, 2, 64, 128), f32),
            pltpu.VMEM((2, 2, 2, 64, 128), f32),
            pltpu.VMEM((2, 2, 64, 128), f32),
            pltpu.VMEM((grps, 8, 128), f32),
            pltpu.VMEM((slabs, 8, 128), f32),
            pltpu.VMEM((2, 64, 128), f32),
            dma((4,)),
            dma((4,)),
            dma((2, 4)),
            dma((2, 4)),
            dma((grps,)),
            dma((grps,)),
            dma((slabs,)),
            dma((slabs,)),
            dma((slabs,)),
            dma((slabs,)),
            dma,
        ],
        compiler_params=pltpu.CompilerParams(
            collective_id=0, has_side_effects=True
        ),
    )(*args)
    spread = result.reshape(slabs, 2, 32, 2, 128).transpose(0, 1, 3, 2, 4)
    return spread.reshape(slabs, 2, 2, 4096)


def solution(mesh):
    return jax.shard_map(
        functools.partial(local, mesh.shape["slab"], mesh.shape["grp"]),
        mesh=mesh,
        in_specs=(
            P("slab", "grp", None, None),
            P("slab", "grp", None, None),
            P("slab", "grp", None, None),
            P("slab", "grp", None, None),
            P(),
            P(),
            P(),
            P("slab", "grp", None, None, None),
        ),
        out_specs=P(None, "grp", None, None),
        check_vma=False,
    )
```

```python
import functools

import jax
import jax.numpy as jnp
from jax import lax
from jax.experimental import pallas as pl
from jax.experimental.pallas import tpu as pltpu
from jax.sharding import PartitionSpec as P

SWEEPS = 8
UNITS = SWEEPS + 2
REACH = SWEEPS // 4

MESH = pl.DeviceIdType.MESH
f32, bf16 = jnp.float32, jnp.bfloat16
highest = lax.Precision.HIGHEST
DOWN_A, UP_A, DOWN_B, UP_B, DOWN_C, UP_C = range(6)


def split(x):
    hi = x.astype(bf16)
    return hi, (x - hi.astype(f32)).astype(bf16)


def mm(a, b, precision=None, across=0):
    return lax.dot_general(
        a, b, (((1,), (across,)), ((), ())), precision=precision, preferred_element_type=f32
    )


def roll(x, by):
    return pltpu.roll(x, by % 128, 1)


def iota(shape, dim):
    return lax.broadcasted_iota(jnp.int32, shape, dim)


def kernel(
    slabs,
    grps,
    dens_hbm,
    slots_hbm,
    neigh_hbm,
    codes_hbm,
    stiff_hbm,
    prolong_hbm,
    penalty_hbm,
    fine_hbm,
    out,
    dens,
    slots,
    neigh,
    codes,
    stiff,
    prolong,
    penalty,
    fine,
    in_sems,
    rho,
    rho_in,
    templ,
    wide,
    ops,
    pack,
    held,
    weights,
    rhs,
    ijac,
    vec,
    part,
    g_up,
    g_down,
    w0,
    resid,
    total,
    top_1,
    top_2,
    done,
    parts,
    rho_ss,
    rho_rs,
    held_ss,
    held_rs,
    top1_ss,
    top1_rs,
    top2_ss,
    top2_rs,
    parts_ss,
    parts_rs,
):
    chunks = 2 * slabs
    q = 64 // chunks
    rows = 2 * q
    pairs = grps // 2
    a = lax.axis_index("slab")
    b = lax.axis_index("grp")
    core = lax.rem(b, 2)
    pair = b // 2
    mine = 2 * a + core
    up_a, down_a = lax.rem(a + 1, slabs), lax.rem(a + slabs - 1, slabs)
    up_b, down_b = lax.rem(b + 1, grps), lax.rem(b + grps - 1, grps)

    loads = [
        pltpu.make_async_copy(src, dst, in_sems.at[i])
        for i, (src, dst) in enumerate(
            (
                (dens_hbm, dens),
                (slots_hbm, slots),
                (neigh_hbm, neigh),
                (codes_hbm, codes),
                (stiff_hbm, stiff),
                (prolong_hbm, prolong),
                (penalty_hbm, penalty),
                (fine_hbm, fine),
            )
        )
    ]
    dens_in, slots_in, neigh_in, codes_in, stiff_in, prolong_in, penalty_in, fine_in = loads
    for load in loads:
        load.start()

    def each(first, last, act):
        def body(d, _):
            act(d)
            return 0

        lax.fori_loop(first, last, body, 0)

    def device(step, d):
        chunk = lax.rem(mine + d, chunks)
        return chunk, (chunk // 2, 2 * lax.rem(pair + step + pairs, pairs) + lax.rem(chunk, 2))

    def along(d):
        return (a, 2 * lax.rem(pair + d, pairs) + core)

    barrier = pltpu.get_barrier_semaphore()

    def greet(where):
        pl.semaphore_signal(barrier, inc=1, device_id=where, device_id_type=MESH)

    steps = [0] + [sign * n for n in range(1, REACH + 1) for sign in (1, -1)]
    for step in steps:
        each(1 if step == 0 else 0, chunks, lambda d: greet(device(step, d)[1]))
    each(REACH + 1, pairs - REACH, lambda d: greet(along(d)))

    left = iota((64, 128), 1) < 64

    dens_in.wait()
    for l in range(4):
        mean = dens[0, l // 2, l % 2, 0]
        for c in range(1, 8):
            mean = mean + dens[0, l // 2, l % 2, c]
        rho[l : l + 1, :] = jnp.full((1, 128), mean * 0.125, f32)
    rho[4:8, :] = jnp.ones((4, 128), f32)

    pl.semaphore_wait(barrier, (2 * REACH + 1) * chunks - 1 + max(0, pairs - 2 * REACH - 1))

    def rho_copy(i, to_a, to_b):
        return pltpu.make_async_remote_copy(
            src_ref=rho,
            dst_ref=rho_in.at[i],
            send_sem=rho_ss.at[i],
            recv_sem=rho_rs.at[i],
            device_id=(to_a, to_b),
            device_id_type=MESH,
        )

    rho_copies = [
        rho_copy(DOWN_A, up_a, b),
        rho_copy(UP_A, down_a, b),
        rho_copy(DOWN_B, a, up_b),
        rho_copy(UP_B, a, down_b),
    ]
    for copy in rho_copies:
        copy.start()

    prolong_in.wait()
    for h in range(2):
        for s in range(8):
            wide[pl.ds(s * 32, 32), h * 64 : h * 64 + 64] = prolong[
                s, pl.ds(h, 32, stride=2), :
            ]
    w_hi, w_lo = split(wide[...].T)
    w_both = jnp.concatenate([w_hi, w_lo], axis=0)
    row, col = iota((256, 256), 0), iota((256, 256), 1)
    same_pair = lax.rem(row, 32) == col // 8
    cell = lax.rem(iota((1, 256), 1), 8)
    slots_in.wait()
    fine_in.wait()
    ys = []
    for l in range(4):
        slot_of = jnp.zeros((1, 256), jnp.int32)
        for c in range(8):
            slot_of = jnp.where(cell == c, slots[0, l // 2, l % 2, c], slot_of)
        pick = jnp.where(same_pair & (row // 32 == slot_of), 1.0, 0.0).astype(bf16)
        ordered = mm(pick, fine[l]).astype(bf16)
        both = mm(w_both, ordered)
        ys.append(both[:128] + both[128:])
    coarse = []
    for m in range(2):
        y0, y1 = ys[2 * m], ys[2 * m + 1]
        coarse.append(
            jnp.where(left, y0[:64], y1[64:]) + roll(jnp.where(left, y1[:64], y0[64:]), 64)
        )
    r128, l128 = iota((128, 128), 0), iota((128, 128), 1)
    order = jnp.where(
        lax.rem(r128 // q, 2) * 64 + (r128 // rows) * q + lax.rem(r128, q) == l128, 1.0, 0.0
    ).astype(bf16)
    hi, lo = split(jnp.concatenate(coarse, axis=0))
    cut = mm(order, hi, across=1) + mm(order, lo, across=1)
    for chunk in range(chunks):
        pack[chunk, :rows, :] = cut[chunk * rows : chunk * rows + rows]

    stiff_in.wait()
    penalty_in.wait()
    eye = iota((64, 64), 0) == iota((64, 64), 1)
    lane64 = iota((64, 128), 1)
    diags = jnp.zeros((64, 128), f32)
    for s in range(24):
        if s < 8:
            p = prolong[s]
            kp = mm(stiff[...], p, highest)
            matrix = mm(p.T, kp, highest)
            templ[s] = matrix
        else:
            matrix = penalty[s - 8]
        column = jnp.sum(jnp.where(eye, matrix, 0.0), axis=1, keepdims=True)
        diags = jnp.where(lane64 == s, column, diags)
        hi, lo = split(matrix)
        two = jnp.concatenate([hi, lo], axis=1)
        for i in range(4):
            ops[i, s * 16 : s * 16 + 16, 0:128] = two[i * 16 : i * 16 + 16]
            ops[i, s * 16 : s * 16 + 16, 128:192] = hi[i * 16 : i * 16 + 16]

    neigh_in.wait()
    codes_in.wait()
    for copy in rho_copies:
        copy.wait()
    lane, half = iota((rows, 128), 1), iota((rows, 128), 0) // q
    tile = jnp.ones((rows, 128), f32)
    face_w = []
    for m in range(2):
        for k in range(2):
            l = 2 * m + k
            own = rho[l : l + 1, :]
            faces = {
                DOWN_A: rho_in[DOWN_A, l : l + 1, :],
                UP_A: rho_in[UP_A, l : l + 1, :],
                DOWN_B: rho_in[DOWN_B, 2 + k : 3 + k, :] if m == 0 else rho[k : k + 1, :],
                UP_B: rho[2 + k : 3 + k, :] if m == 0 else rho_in[UP_B, k : k + 1, :],
                (UP_C if k == 0 else DOWN_C): rho[2 * m + 1 - k : 2 * m + 2 - k, :],
            }
            for c in range(8):
                at = (half == k) & (lane == m * 64 + slots[0, m, k, c])
                tile = jnp.where(at, dens[0, m, k, c], tile)
            face_w.append({})
            for face, other in faces.items():
                present = (neigh[0, m, k, face] >= 0).astype(f32)
                face_w[l][face] = 2.0 / (own + other) * present
    tile = 1.0 / tile
    for m in range(2):
        for k in range(2):
            for face in range(6):
                code = codes[0, m, k, face].astype(f32)
                weight = face_w[2 * m + k].get(face, jnp.zeros((1, 128), f32))
                tile = jnp.where((half == k) & (lane == m * 64 + 8 + face), code, tile)
                tile = jnp.where((half == k) & (lane == m * 64 + 14 + face), weight, tile)
    for chunk in range(chunks):
        pack[chunk, rows:, :] = tile

    def held_copy(n, d):
        chunk, where = device(steps[n], d)
        return pltpu.make_async_remote_copy(
            src_ref=pack.at[chunk],
            dst_ref=held.at[2 * REACH - 2 * steps[n] + core, a],
            send_sem=held_ss.at[n, d],
            recv_sem=held_rs.at[n, d],
            device_id=where,
            device_id_type=MESH,
        )

    for n in reversed(range(len(steps))):
        each(1 if n == 0 else 0, chunks, lambda d: held_copy(n, d).start())
    held[2 * REACH + core, a] = pack[mine]

    top = jnp.zeros((1, 1), f32)
    for m in range(2):
        for k in range(2):
            diag = jnp.zeros((64, 64), f32)
            for c in range(8):
                weight = 1.0 / jnp.full((1, 64), dens[0, m, k, c], f32)
                diag = diag + weight * templ[slots[0, m, k, c]]
            extent = jnp.zeros((64, 64), f32)
            for face, weight in face_w[2 * m + k].items():
                block = weight[:, :64] * penalty[codes[0, m, k, face]]
                diag = diag + block
                extent = extent + jnp.abs(block)
            jac = jnp.sum(jnp.where(eye, diag, 0.0), axis=1, keepdims=True)
            sums = jnp.sum(jnp.abs(diag) + extent, axis=1, keepdims=True)
            top = jnp.maximum(top, jnp.max(sums / jac, axis=0, keepdims=True))

    top_1[0] = jnp.broadcast_to(top, (8, 128))

    def top1_copy(d):
        return pltpu.make_async_remote_copy(
            src_ref=top_1.at[0],
            dst_ref=top_1.at[d],
            send_sem=top1_ss.at[d],
            recv_sem=top1_rs.at[d],
            device_id=device(0, d)[1],
            device_id_type=MESH,
        )

    def top2_copy(d):
        return pltpu.make_async_remote_copy(
            src_ref=top_2.at[0],
            dst_ref=top_2.at[d],
            send_sem=top2_ss.at[d],
            recv_sem=top2_rs.at[d],
            device_id=along(d),
            device_id_type=MESH,
        )

    each(1, chunks, lambda d: top1_copy(d).start())

    for n in range(len(steps)):
        each(1 if n == 0 else 0, chunks, lambda d: held_copy(n, d).wait())
    code16 = iota((16, 128), 0).astype(f32)

    def unpack(j, _):
        got = held[j]
        x = got[:, :rows, :].reshape(64, 128).T
        x = jnp.concatenate([x[:64], x[64:]], axis=1)
        meta = got[:, rows:, :].reshape(64, 128).T
        meta = jnp.concatenate([meta[0:32], meta[64:96]], axis=1)
        weights[j, 0:8, :] = meta[0:8]
        summed = jnp.zeros((16, 128), f32)
        for face in range(6):
            hot = jnp.where(
                code16 == meta[8 + face : 9 + face], meta[14 + face : 15 + face], 0.0
            )
            weights[j, 8 + 16 * face : 24 + 16 * face, :] = hot
            summed = summed + hot
        table = jnp.concatenate([meta[0:8], summed, jnp.zeros((104, 128), f32)], axis=0)
        over = 1.0 / mm(diags, table, highest)
        rhs[j] = x
        ijac[j] = over
        vec[j] = x * over
        return 0

    lax.fori_loop(0, UNITS, unpack, 0)

    each(1, chunks, lambda d: top1_copy(d).wait())
    top_2[0] = jnp.max(top_1[...], axis=0)
    each(1, pairs, lambda d: top2_copy(d).start())

    def products(t):
        def two(i, _):
            j = t // 2 + 2 * i
            hi, lo = split(jnp.concatenate([vec[j], vec[j + 1]], axis=1))
            stack = jnp.concatenate([hi, hi, lo], axis=0)
            for n in range(4):
                every = mm(ops[n], stack)
                at = slice(n * 16, n * 16 + 16)
                for u in range(2):
                    y = every[:, u * 128 : u * 128 + 128]
                    result = jnp.zeros((16, 128), f32)
                    for s in range(8):
                        result = result + weights[j + u, s : s + 1, :] * y[s * 16 : s * 16 + 16]
                    g = []
                    for face in range(6):
                        flux = jnp.zeros((16, 128), f32)
                        for c in range(16):
                            w = 8 + 16 * face + c
                            flux = flux + (
                                weights[j + u, w : w + 1, :] * y[128 + c * 16 : 144 + c * 16]
                            )
                        g.append(flux)
                        result = result + flux
                    result = result - roll(g[UP_A], rows) - roll(g[DOWN_A], -rows)
                    part[j + u, at, :] = result - roll(g[UP_C], q) - roll(g[DOWN_C], -q)
                    g_up[j + u, at, :] = g[UP_B]
                    g_down[j + u, at, :] = g[DOWN_B]
            return 0

        lax.fori_loop(0, SWEEPS // 2 + 1 - t // 2, two, 0)

    def applied(t, use):
        def one(j, _):
            below, above = jnp.maximum(j - 1, 0), jnp.minimum(j + 1, UNITS - 1)
            low = roll(jnp.where(left, g_up[j], g_up[below]), 64)
            high = roll(jnp.where(left, g_down[above], g_down[j]), 64)
            use(j, part[j] - low - high)
            return 0

        lax.fori_loop((t + 1) // 2, UNITS - (t + 1) // 2, one, 0)

    def keep_first(j, value):
        w0[j] = value
        vec[j] = value * ijac[j]

    products(0)
    applied(0, keep_first)
    products(1)
    each(1, pairs, lambda d: top2_copy(d).wait())
    upper = jnp.max(top_2[...], axis=0)[0:1, :]

    lower = upper / 10.0
    centre_val = 0.5 * (upper + lower)
    half_width = 0.5 * (upper - lower)
    sigma = centre_val / half_width
    over_centre = 1.0 / centre_val
    damp0 = 1.0 / sigma
    damp1 = 1.0 / (2.0 * sigma - damp0)
    keep1, gain1 = damp1 * damp0, 2.0 * damp1 / half_width
    damp2 = 1.0 / (2.0 * sigma - damp1)
    keep2, gain2 = damp2 * damp1, 2.0 * damp2 / half_width

    def combine(j, second):
        over, first = ijac[j], w0[j]
        update0 = rhs[j] * over * over_centre
        resid1 = rhs[j] - first * over_centre
        update1 = keep1 * update0 + gain1 * (resid1 * over)
        both = (keep1 * over_centre) * first + gain1 * (first - over_centre * second)
        resid2 = resid1 - both
        update2 = keep2 * update1 + gain2 * (resid2 * over)
        resid[j] = resid2
        total[j] = update0 + update1 + update2
        vec[j] = update2

    applied(1, combine)

    def sweep(t, damp):
        damp_next = 1.0 / (2.0 * sigma - damp)
        keep, gain = damp_next * damp, 2.0 * damp_next / half_width

        def step(j, value):
            now = resid[j] - value
            resid[j] = now
            update = keep * vec[j] + gain * (now * ijac[j])
            total[j] = total[j] + update
            vec[j] = update

        products(t)
        applied(t, step)
        return damp_next

    lax.fori_loop(2, SWEEPS, sweep, damp2)

    for u in range(2):
        x = total[2 * REACH + u]
        done[u] = jnp.concatenate([x[:, :64], x[:, 64:]], axis=0).T

    def parts_copy(d):
        chunk, where = device(0, d)
        return pltpu.make_async_remote_copy(
            src_ref=done.at[lax.rem(chunk, 2)],
            dst_ref=parts.at[mine],
            send_sem=parts_ss.at[d],
            recv_sem=parts_rs.at[d],
            device_id=where,
            device_id_type=MESH,
        )

    each(1, chunks, lambda d: parts_copy(d).start())
    parts[mine] = done[core]
    each(1, chunks, lambda d: parts_copy(d).wait())

    even = lax.rem(iota((64, 128), 0), 2) == 0

    def place(i, _):
        at = pl.ds(pl.multiple_of(i * rows, rows), rows)
        hi, lo = split(parts[:, at, :].reshape(128, 128).T)
        x = mm(hi, order) + mm(lo, order)
        for m in range(2):
            own = x[m * 64 : m * 64 + 64]
            turned = roll(own, 64)
            moved = jnp.where(even, pltpu.roll(turned, 63, 0), pltpu.roll(turned, 1, 0))
            out[i, m] = jnp.where(even == left, own, moved)
        return 0

    lax.fori_loop(0, slabs, place, 0)


def local(slabs, grps, dens, slots, neigh, codes, stiff, prolong, penalty, fine):
    x = fine.reshape(4, 8, 32, 128).transpose(0, 2, 1, 3).reshape(4, 256, 128)
    smem, vmem = pltpu.SMEM, pltpu.VMEM
    args = (dens, slots, neigh, codes, stiff, prolong, penalty, x)
    dma = pltpu.SemaphoreType.DMA
    chunks, pairs = 2 * slabs, grps // 2
    rows = 128 // chunks
    reach = 2 * REACH + 1
    columns = pltpu.VMEM((UNITS, 64, 128), f32)
    result = pl.pallas_call(
        functools.partial(kernel, slabs, grps),
        out_shape=jax.ShapeDtypeStruct((slabs, 2, 64, 128), f32),
        in_specs=[pl.BlockSpec(memory_space=pl.ANY)] * 8,
        out_specs=pl.BlockSpec(memory_space=pltpu.VMEM),
        scratch_shapes=[
            *(space(v.shape, v.dtype) for space, v in zip([smem] * 4 + [vmem] * 4, args)),
            dma((8,)),
            pltpu.VMEM((8, 128), f32),
            pltpu.VMEM((4, 8, 128), f32),
            pltpu.VMEM((8, 64, 64), f32),
            pltpu.VMEM((256, 128), f32),
            pltpu.VMEM((4, 384, 192), bf16),
            pltpu.VMEM((chunks, 2 * rows, 128), f32),
            pltpu.VMEM((UNITS, slabs, 2 * rows, 128), f32),
            pltpu.VMEM((UNITS, 104, 128), f32),
            *[columns] * 9,
            pltpu.VMEM((chunks, 8, 128), f32),
            pltpu.VMEM((pairs, 8, 128), f32),
            pltpu.VMEM((2, 64, 128), f32),
            pltpu.VMEM((chunks, 64, 128), f32),
            dma((4,)),
            dma((4,)),
            dma((reach, chunks)),
            dma((reach, chunks)),
            dma((chunks,)),
            dma((chunks,)),
            dma((pairs,)),
            dma((pairs,)),
            dma((chunks,)),
            dma((chunks,)),
        ],
        compiler_params=pltpu.CompilerParams(collective_id=0, has_side_effects=True),
    )(*args)
    spread = result.reshape(slabs, 2, 32, 2, 128).transpose(0, 1, 3, 2, 4)
    return spread.reshape(slabs, 2, 2, 4096)


def solution(mesh):
    return jax.shard_map(
        functools.partial(local, mesh.shape["slab"], mesh.shape["grp"]),
        mesh=mesh,
        in_specs=(
            P("slab", "grp", None, None),
            P("slab", "grp", None, None),
            P("slab", "grp", None, None),
            P("slab", "grp", None, None),
            P(),
            P(),
            P(),
            P("slab", "grp", None, None, None),
        ),
        out_specs=P(None, "grp", None, None),
        check_vma=False,
    )
```

```python
import functools

import jax
import jax.numpy as jnp
from jax import lax
from jax.experimental import pallas as pl
from jax.experimental.pallas import tpu as pltpu
from jax.sharding import PartitionSpec as P

SWEEPS = 8
REACH = 1
SPAN = 4 * REACH
UNITS = 4 * REACH + 2

MESH = pl.DeviceIdType.MESH
f32, bf16 = jnp.float32, jnp.bfloat16
highest = lax.Precision.HIGHEST
DOWN_A, UP_A, DOWN_B, UP_B, DOWN_C, UP_C = range(6)


def split(x):
    hi = x.astype(bf16)
    return hi, (x - hi.astype(f32)).astype(bf16)


def mm(a, b, precision=None, across=0):
    return lax.dot_general(
        a, b, (((1,), (across,)), ((), ())), precision=precision, preferred_element_type=f32
    )


def roll(x, by):
    return pltpu.roll(x, by % 128, 1)


def iota(shape, dim):
    return lax.broadcasted_iota(jnp.int32, shape, dim)


def kernel(
    slabs,
    grps,
    dens_hbm,
    slots_hbm,
    neigh_hbm,
    codes_hbm,
    stiff_hbm,
    prolong_hbm,
    penalty_hbm,
    fine_hbm,
    out,
    dens,
    slots,
    neigh,
    codes,
    stiff,
    prolong,
    penalty,
    fine,
    in_sems,
    rho,
    rho_in,
    templ,
    wide,
    ops,
    pack,
    held,
    weights,
    rhs,
    ijac,
    vec,
    part,
    g_up,
    g_down,
    w0,
    resid,
    total,
    top_1,
    top_2,
    edge,
    edge_in,
    done,
    parts,
    rho_ss,
    rho_rs,
    held_ss,
    held_rs,
    top1_ss,
    top1_rs,
    top2_ss,
    top2_rs,
    edge_ss,
    edge_rs,
    parts_ss,
    parts_rs,
):
    chunks = 2 * slabs
    q = 64 // chunks
    rows = 2 * q
    pairs = grps // 2
    a = lax.axis_index("slab")
    b = lax.axis_index("grp")
    core = lax.rem(b, 2)
    pair = b // 2
    mine = 2 * a + core
    up_a, down_a = lax.rem(a + 1, slabs), lax.rem(a + slabs - 1, slabs)
    up_b, down_b = lax.rem(b + 1, grps), lax.rem(b + grps - 1, grps)

    loads = [
        pltpu.make_async_copy(src, dst, in_sems.at[i])
        for i, (src, dst) in enumerate(
            (
                (dens_hbm, dens),
                (slots_hbm, slots),
                (neigh_hbm, neigh),
                (codes_hbm, codes),
                (stiff_hbm, stiff),
                (prolong_hbm, prolong),
                (penalty_hbm, penalty),
                (fine_hbm, fine),
            )
        )
    ]
    dens_in, slots_in, neigh_in, codes_in, stiff_in, prolong_in, penalty_in, fine_in = loads
    for load in loads:
        load.start()

    def each(first, last, act):
        def body(d, _):
            act(d)
            return 0

        lax.fori_loop(first, last, body, 0)

    def device(step, d):
        chunk = lax.rem(mine + d, chunks)
        return chunk, (chunk // 2, 2 * lax.rem(pair + step + pairs, pairs) + lax.rem(chunk, 2))

    def along(d):
        return (a, 2 * lax.rem(pair + d, pairs) + core)

    barrier = pltpu.get_barrier_semaphore()

    def greet(where):
        pl.semaphore_signal(barrier, inc=1, device_id=where, device_id_type=MESH)

    steps = [0] + [sign * n for n in range(1, REACH + 1) for sign in (1, -1)]
    for step in steps:
        each(1 if step == 0 else 0, chunks, lambda d: greet(device(step, d)[1]))
    each(REACH + 1, pairs - REACH, lambda d: greet(along(d)))

    left = iota((64, 128), 1) < 64

    dens_in.wait()
    for l in range(4):
        mean = dens[0, l // 2, l % 2, 0]
        for c in range(1, 8):
            mean = mean + dens[0, l // 2, l % 2, c]
        rho[l : l + 1, :] = jnp.full((1, 128), mean * 0.125, f32)
    rho[4:8, :] = jnp.ones((4, 128), f32)

    pl.semaphore_wait(barrier, (2 * REACH + 1) * chunks - 1 + max(0, pairs - 2 * REACH - 1))

    def rho_copy(i, to_a, to_b):
        return pltpu.make_async_remote_copy(
            src_ref=rho,
            dst_ref=rho_in.at[i],
            send_sem=rho_ss.at[i],
            recv_sem=rho_rs.at[i],
            device_id=(to_a, to_b),
            device_id_type=MESH,
        )

    rho_copies = [
        rho_copy(DOWN_A, up_a, b),
        rho_copy(UP_A, down_a, b),
        rho_copy(DOWN_B, a, up_b),
        rho_copy(UP_B, a, down_b),
    ]
    for copy in rho_copies:
        copy.start()

    prolong_in.wait()
    for h in range(2):
        for s in range(8):
            wide[pl.ds(s * 32, 32), h * 64 : h * 64 + 64] = prolong[
                s, pl.ds(h, 32, stride=2), :
            ]
    w_hi, w_lo = split(wide[...].T)
    w_both = jnp.concatenate([w_hi, w_lo], axis=0)
    row, col = iota((256, 256), 0), iota((256, 256), 1)
    same_pair = lax.rem(row, 32) == col // 8
    cell = lax.rem(iota((1, 256), 1), 8)
    slots_in.wait()
    fine_in.wait()
    ys = []
    for l in range(4):
        slot_of = jnp.zeros((1, 256), jnp.int32)
        for c in range(8):
            slot_of = jnp.where(cell == c, slots[0, l // 2, l % 2, c], slot_of)
        pick = jnp.where(same_pair & (row // 32 == slot_of), 1.0, 0.0).astype(bf16)
        ordered = mm(pick, fine[l]).astype(bf16)
        both = mm(w_both, ordered)
        ys.append(both[:128] + both[128:])
    coarse = []
    for m in range(2):
        y0, y1 = ys[2 * m], ys[2 * m + 1]
        coarse.append(
            jnp.where(left, y0[:64], y1[64:]) + roll(jnp.where(left, y1[:64], y0[64:]), 64)
        )
    r128, l128 = iota((128, 128), 0), iota((128, 128), 1)
    order = jnp.where(
        lax.rem(r128 // q, 2) * 64 + (r128 // rows) * q + lax.rem(r128, q) == l128, 1.0, 0.0
    ).astype(bf16)
    hi, lo = split(jnp.concatenate(coarse, axis=0))
    cut = mm(order, hi, across=1) + mm(order, lo, across=1)
    for chunk in range(chunks):
        pack[chunk, :rows, :] = cut[chunk * rows : chunk * rows + rows]

    stiff_in.wait()
    penalty_in.wait()
    eye = iota((64, 64), 0) == iota((64, 64), 1)
    lane64 = iota((64, 128), 1)
    diags = jnp.zeros((64, 128), f32)
    for s in range(24):
        if s < 8:
            p = prolong[s]
            kp = mm(stiff[...], p, highest)
            matrix = mm(p.T, kp, highest)
            templ[s] = matrix
        else:
            matrix = penalty[s - 8]
        column = jnp.sum(jnp.where(eye, matrix, 0.0), axis=1, keepdims=True)
        diags = jnp.where(lane64 == s, column, diags)
        hi, lo = split(matrix)
        two = jnp.concatenate([hi, lo], axis=1)
        for i in range(2):
            ops[i, s * 32 : s * 32 + 32, 0:128] = two[i * 32 : i * 32 + 32]
            ops[i, s * 32 : s * 32 + 32, 128:192] = hi[i * 32 : i * 32 + 32]

    neigh_in.wait()
    codes_in.wait()
    for copy in rho_copies:
        copy.wait()
    lane, half = iota((rows, 128), 1), iota((rows, 128), 0) // q
    tile = jnp.ones((rows, 128), f32)
    face_w = []
    for m in range(2):
        for k in range(2):
            l = 2 * m + k
            own = rho[l : l + 1, :]
            faces = {
                DOWN_A: rho_in[DOWN_A, l : l + 1, :],
                UP_A: rho_in[UP_A, l : l + 1, :],
                DOWN_B: rho_in[DOWN_B, 2 + k : 3 + k, :] if m == 0 else rho[k : k + 1, :],
                UP_B: rho[2 + k : 3 + k, :] if m == 0 else rho_in[UP_B, k : k + 1, :],
                (UP_C if k == 0 else DOWN_C): rho[2 * m + 1 - k : 2 * m + 2 - k, :],
            }
            for c in range(8):
                at = (half == k) & (lane == m * 64 + slots[0, m, k, c])
                tile = jnp.where(at, dens[0, m, k, c], tile)
            face_w.append({})
            for face, other in faces.items():
                present = (neigh[0, m, k, face] >= 0).astype(f32)
                face_w[l][face] = 2.0 / (own + other) * present
    tile = 1.0 / tile
    for m in range(2):
        for k in range(2):
            for face in range(6):
                code = codes[0, m, k, face].astype(f32)
                weight = face_w[2 * m + k].get(face, jnp.zeros((1, 128), f32))
                tile = jnp.where((half == k) & (lane == m * 64 + 8 + face), code, tile)
                tile = jnp.where((half == k) & (lane == m * 64 + 14 + face), weight, tile)
    for chunk in range(chunks):
        pack[chunk, rows:, :] = tile

    def held_copy(n, d):
        chunk, where = device(steps[n], d)
        return pltpu.make_async_remote_copy(
            src_ref=pack.at[chunk],
            dst_ref=held.at[2 * REACH - 2 * steps[n] + core, a],
            send_sem=held_ss.at[n, d],
            recv_sem=held_rs.at[n, d],
            device_id=where,
            device_id_type=MESH,
        )

    for n in reversed(range(len(steps))):
        each(1 if n == 0 else 0, chunks, lambda d: held_copy(n, d).start())
    held[2 * REACH + core, a] = pack[mine]

    top = jnp.zeros((1, 1), f32)
    for m in range(2):
        for k in range(2):
            diag = jnp.zeros((64, 64), f32)
            for c in range(8):
                weight = 1.0 / jnp.full((1, 64), dens[0, m, k, c], f32)
                diag = diag + weight * templ[slots[0, m, k, c]]
            extent = jnp.zeros((64, 64), f32)
            for face, weight in face_w[2 * m + k].items():
                block = weight[:, :64] * penalty[codes[0, m, k, face]]
                diag = diag + block
                extent = extent + jnp.abs(block)
            jac = jnp.sum(jnp.where(eye, diag, 0.0), axis=1, keepdims=True)
            sums = jnp.sum(jnp.abs(diag) + extent, axis=1, keepdims=True)
            top = jnp.maximum(top, jnp.max(sums / jac, axis=0, keepdims=True))

    top_1[0] = jnp.broadcast_to(top, (8, 128))

    def top1_copy(d):
        return pltpu.make_async_remote_copy(
            src_ref=top_1.at[0],
            dst_ref=top_1.at[d],
            send_sem=top1_ss.at[d],
            recv_sem=top1_rs.at[d],
            device_id=device(0, d)[1],
            device_id_type=MESH,
        )

    def top2_copy(d):
        return pltpu.make_async_remote_copy(
            src_ref=top_2.at[0],
            dst_ref=top_2.at[d],
            send_sem=top2_ss.at[d],
            recv_sem=top2_rs.at[d],
            device_id=along(d),
            device_id_type=MESH,
        )

    each(1, chunks, lambda d: top1_copy(d).start())

    for n in range(len(steps)):
        each(1 if n == 0 else 0, chunks, lambda d: held_copy(n, d).wait())
    code16 = iota((16, 128), 0).astype(f32)

    def unpack(j, _):
        got = held[j]
        x = got[:, :rows, :].reshape(64, 128).T
        x = jnp.concatenate([x[:64], x[64:]], axis=1)
        meta = got[:, rows:, :].reshape(64, 128).T
        meta = jnp.concatenate([meta[0:32], meta[64:96]], axis=1)
        weights[j] = meta
        summed = jnp.zeros((16, 128), f32)
        for face in range(6):
            summed = summed + jnp.where(
                code16 == meta[8 + face : 9 + face], meta[14 + face : 15 + face], 0.0
            )
        table = jnp.concatenate([meta[0:8], summed, jnp.zeros((104, 128), f32)], axis=0)
        over = 1.0 / mm(diags, table, highest)
        rhs[j] = x
        ijac[j] = over
        vec[j] = x * over
        return 0

    lax.fori_loop(0, UNITS, unpack, 0)

    each(1, chunks, lambda d: top1_copy(d).wait())
    top_2[0] = jnp.max(top_1[...], axis=0)
    each(1, pairs, lambda d: top2_copy(d).start())

    def products(t):
        def two(i, _):
            j = t // 2 + 2 * i
            hi, lo = split(jnp.concatenate([vec[j], vec[j + 1]], axis=1))
            stack = jnp.concatenate([hi, hi, lo], axis=0)
            for n in range(2):
                every = mm(ops[n], stack)
                at = slice(n * 32, n * 32 + 32)
                for u in range(2):
                    y = every[:, u * 128 : u * 128 + 128]
                    w = weights.at[j + u]
                    result = w[0:1, :] * y[0:32]
                    for s in range(1, 8):
                        result = result + w[s : s + 1, :] * y[s * 32 : s * 32 + 32]
                    g = []
                    for face in range(6):
                        code = jnp.broadcast_to(w[8 + face : 9 + face, :], (32, 128))
                        flux = y[256:288]
                        for c in range(1, 16):
                            flux = jnp.where(code == c, y[256 + c * 32 : 288 + c * 32], flux)
                        g.append(w[14 + face : 15 + face, :] * flux)
                        result = result + g[face]
                    result = result - roll(g[UP_A], rows) - roll(g[DOWN_A], -rows)
                    part[j + u, at, :] = result - roll(g[UP_C], q) - roll(g[DOWN_C], -q)
                    g_up[j + u, at, :] = g[UP_B]
                    g_down[j + u, at, :] = g[DOWN_B]
            return 0

        lax.fori_loop(0, UNITS // 2 - t // 2, two, 0)

    def applied(t, use):
        def one(j, _):
            below, above = jnp.maximum(j - 1, 0), jnp.minimum(j + 1, UNITS - 1)
            low = roll(jnp.where(left, g_up[j], g_up[below]), 64)
            high = roll(jnp.where(left, g_down[above], g_down[j]), 64)
            use(j, part[j] - low - high)
            return 0

        lax.fori_loop((t + 1) // 2, UNITS - (t + 1) // 2, one, 0)

    def keep_first(j, value):
        w0[j] = value
        vec[j] = value * ijac[j]

    products(0)
    applied(0, keep_first)
    products(1)
    each(1, pairs, lambda d: top2_copy(d).wait())
    upper = jnp.max(top_2[...], axis=0)[0:1, :]

    lower = upper / 10.0
    centre_val = 0.5 * (upper + lower)
    half_width = 0.5 * (upper - lower)
    sigma = centre_val / half_width
    over_centre = 1.0 / centre_val
    damp0 = 1.0 / sigma
    damp1 = 1.0 / (2.0 * sigma - damp0)
    keep1, gain1 = damp1 * damp0, 2.0 * damp1 / half_width
    damp2 = 1.0 / (2.0 * sigma - damp1)
    keep2, gain2 = damp2 * damp1, 2.0 * damp2 / half_width

    def combine(j, second):
        over, first = ijac[j], w0[j]
        update0 = rhs[j] * over * over_centre
        resid1 = rhs[j] - first * over_centre
        update1 = keep1 * update0 + gain1 * (resid1 * over)
        both = (keep1 * over_centre) * first + gain1 * (first - over_centre * second)
        resid2 = resid1 - both
        update2 = keep2 * update1 + gain2 * (resid2 * over)
        resid[j] = resid2
        total[j] = update0 + update1 + update2
        vec[j] = update2

    applied(1, combine)

    def sweep(t, damp):
        damp_next = 1.0 / (2.0 * sigma - damp)
        keep, gain = damp_next * damp, 2.0 * damp_next / half_width

        def step(j, value):
            now = resid[j] - value
            resid[j] = now
            update = keep * vec[j] + gain * (now * ijac[j])
            total[j] = total[j] + update
            vec[j] = update

        products(t)
        applied(t, step)
        return damp_next

    damp = lax.fori_loop(2, SPAN, sweep, damp2)

    edge[0] = vec[2 * REACH : 2 * REACH + 2]
    edge[1] = resid[2 * REACH : 2 * REACH + 2]

    def edge_copy(side, d):
        return pltpu.make_async_remote_copy(
            src_ref=edge,
            dst_ref=edge_in.at[side],
            send_sem=edge_ss.at[side],
            recv_sem=edge_rs.at[side],
            device_id=along(d),
            device_id_type=MESH,
        )

    edge_copies = [edge_copy(0, 1), edge_copy(1, pairs - 1)]
    for copy in edge_copies:
        copy.start()
    for copy in edge_copies:
        copy.wait()
    for side in range(2):
        vec[4 * side : 4 * side + 2] = edge_in[side, 0]
        resid[4 * side : 4 * side + 2] = edge_in[side, 1]
    lax.fori_loop(0, SWEEPS - SPAN, sweep, damp)

    for u in range(2):
        x = total[2 * REACH + u]
        done[u] = jnp.concatenate([x[:, :64], x[:, 64:]], axis=0).T

    def parts_copy(d):
        chunk, where = device(0, d)
        return pltpu.make_async_remote_copy(
            src_ref=done.at[lax.rem(chunk, 2)],
            dst_ref=parts.at[mine],
            send_sem=parts_ss.at[d],
            recv_sem=parts_rs.at[d],
            device_id=where,
            device_id_type=MESH,
        )

    each(1, chunks, lambda d: parts_copy(d).start())
    parts[mine] = done[core]
    each(1, chunks, lambda d: parts_copy(d).wait())

    even = lax.rem(iota((64, 128), 0), 2) == 0

    def place(i, _):
        at = pl.ds(pl.multiple_of(i * rows, rows), rows)
        hi, lo = split(parts[:, at, :].reshape(128, 128).T)
        x = mm(hi, order) + mm(lo, order)
        for m in range(2):
            own = x[m * 64 : m * 64 + 64]
            turned = roll(own, 64)
            moved = jnp.where(even, pltpu.roll(turned, 63, 0), pltpu.roll(turned, 1, 0))
            out[i, m] = jnp.where(even == left, own, moved)
        return 0

    lax.fori_loop(0, slabs, place, 0)


def local(slabs, grps, dens, slots, neigh, codes, stiff, prolong, penalty, fine):
    x = fine.reshape(4, 8, 32, 128).transpose(0, 2, 1, 3).reshape(4, 256, 128)
    smem, vmem = pltpu.SMEM, pltpu.VMEM
    args = (dens, slots, neigh, codes, stiff, prolong, penalty, x)
    dma = pltpu.SemaphoreType.DMA
    chunks, pairs = 2 * slabs, grps // 2
    rows = 128 // chunks
    reach = 2 * REACH + 1
    columns = pltpu.VMEM((UNITS, 64, 128), f32)
    result = pl.pallas_call(
        functools.partial(kernel, slabs, grps),
        out_shape=jax.ShapeDtypeStruct((slabs, 2, 64, 128), f32),
        in_specs=[pl.BlockSpec(memory_space=pl.ANY)] * 8,
        out_specs=pl.BlockSpec(memory_space=pltpu.VMEM),
        scratch_shapes=[
            *(space(v.shape, v.dtype) for space, v in zip([smem] * 4 + [vmem] * 4, args)),
            dma((8,)),
            pltpu.VMEM((8, 128), f32),
            pltpu.VMEM((4, 8, 128), f32),
            pltpu.VMEM((8, 64, 64), f32),
            pltpu.VMEM((256, 128), f32),
            pltpu.VMEM((2, 768, 192), bf16),
            pltpu.VMEM((chunks, 2 * rows, 128), f32),
            pltpu.VMEM((UNITS, slabs, 2 * rows, 128), f32),
            pltpu.VMEM((UNITS, 32, 128), f32),
            *[columns] * 9,
            pltpu.VMEM((chunks, 8, 128), f32),
            pltpu.VMEM((pairs, 8, 128), f32),
            pltpu.VMEM((2, 2, 64, 128), f32),
            pltpu.VMEM((2, 2, 2, 64, 128), f32),
            pltpu.VMEM((2, 64, 128), f32),
            pltpu.VMEM((chunks, 64, 128), f32),
            dma((4,)),
            dma((4,)),
            dma((reach, chunks)),
            dma((reach, chunks)),
            dma((chunks,)),
            dma((chunks,)),
            dma((pairs,)),
            dma((pairs,)),
            dma((2,)),
            dma((2,)),
            dma((chunks,)),
            dma((chunks,)),
        ],
        compiler_params=pltpu.CompilerParams(collective_id=0, has_side_effects=True),
    )(*args)
    spread = result.reshape(slabs, 2, 32, 2, 128).transpose(0, 1, 3, 2, 4)
    return spread.reshape(slabs, 2, 2, 4096)


def solution(mesh):
    return jax.shard_map(
        functools.partial(local, mesh.shape["slab"], mesh.shape["grp"]),
        mesh=mesh,
        in_specs=(
            P("slab", "grp", None, None),
            P("slab", "grp", None, None),
            P("slab", "grp", None, None),
            P("slab", "grp", None, None),
            P(),
            P(),
            P(),
            P("slab", "grp", None, None, None),
        ),
        out_specs=P(None, "grp", None, None),
        check_vma=False,
    )
```

```python
import functools

import jax
import jax.numpy as jnp
from jax import lax
from jax.experimental import pallas as pl
from jax.experimental.pallas import tpu as pltpu
from jax.sharding import PartitionSpec as P

SWEEPS = 8
REACH = 1
SPAN = 4 * REACH
UNITS = 4 * REACH + 2

MESH = pl.DeviceIdType.MESH
f32, bf16 = jnp.float32, jnp.bfloat16
highest = lax.Precision.HIGHEST
DOWN_A, UP_A, DOWN_B, UP_B, DOWN_C, UP_C = range(6)


def split(x):
    hi = x.astype(bf16)
    return hi, (x - hi.astype(f32)).astype(bf16)


def mm(a, b, precision=None, across=0):
    return lax.dot_general(
        a, b, (((1,), (across,)), ((), ())), precision=precision, preferred_element_type=f32
    )


def roll(x, by):
    return pltpu.roll(x, by % 128, 1)


def iota(shape, dim):
    return lax.broadcasted_iota(jnp.int32, shape, dim)


def kernel(
    slabs,
    grps,
    dens_hbm,
    slots_hbm,
    neigh_hbm,
    codes_hbm,
    stiff_hbm,
    prolong_hbm,
    penalty_hbm,
    fine_hbm,
    out,
    dens,
    slots,
    neigh,
    codes,
    stiff,
    prolong,
    penalty,
    fine,
    in_sems,
    rho,
    rho_in,
    templ,
    wide,
    ops,
    pack,
    held,
    base,
    more,
    vec,
    part,
    g_up,
    g_down,
    w0,
    resid,
    total,
    top_1,
    top_2,
    top_3,
    edge,
    edge_in,
    done,
    parts,
    ready,
    out_sems,
    rho_ss,
    rho_rs,
    held_ss,
    held_rs,
    top1_ss,
    top1_rs,
    top2_ss,
    top2_rs,
    top3_sems,
    base_ss,
    base_rs,
    edge_ss,
    edge_rs,
    parts_ss,
    parts_rs,
):
    chunks = 2 * slabs
    q = 64 // chunks
    rows = 2 * q
    pairs = grps // 2
    a = lax.axis_index("slab")
    b = lax.axis_index("grp")
    core = lax.rem(b, 2)
    pair = b // 2
    mine = 2 * a + core
    up_a, down_a = lax.rem(a + 1, slabs), lax.rem(a + slabs - 1, slabs)
    up_b, down_b = lax.rem(b + 1, grps), lax.rem(b + grps - 1, grps)

    loads = [
        pltpu.make_async_copy(src, dst, in_sems.at[i])
        for i, (src, dst) in enumerate(
            (
                (dens_hbm, dens),
                (slots_hbm, slots),
                (neigh_hbm, neigh),
                (codes_hbm, codes),
                (stiff_hbm, stiff),
                (prolong_hbm, prolong),
                (penalty_hbm, penalty),
                (fine_hbm, fine),
            )
        )
    ]
    dens_in, slots_in, neigh_in, codes_in, stiff_in, prolong_in, penalty_in, fine_in = loads
    for load in loads:
        load.start()

    def each(first, last, act):
        def body(d, _):
            act(d)
            return 0

        lax.fori_loop(first, last, body, 0)

    def device(d):
        chunk = lax.rem(mine + d, chunks)
        return chunk, (chunk // 2, 2 * pair + lax.rem(chunk, 2))

    def along(d):
        return (a, 2 * lax.rem(pair + d, pairs) + core)

    near = pairs // 2

    def around(d):
        return (a, 2 * (pair // near * near + lax.rem(lax.rem(pair, near) + d, near)) + core)

    opposite = along(near)
    start, weights = base.at[:, 0:64], base.at[:, 64:88]
    rhs, ijac = more.at[:, 0:64], more.at[:, 64:128]

    barrier = pltpu.get_barrier_semaphore()

    def greet(where):
        pl.semaphore_signal(barrier, inc=1, device_id=where, device_id_type=MESH)

    for d in range(1, chunks):
        greet(device(d)[1])
    greet(along(1))
    greet(along(pairs - 1))
    for d in range(1, near):
        greet(around(d))
    greet(opposite)
    greet((a, lax.rem(b + grps - 1 + 2 * core, grps)))

    left = iota((64, 128), 1) < 64

    dens_in.wait()
    for l in range(4):
        mean = dens[0, l // 2, l % 2, 0]
        for c in range(1, 8):
            mean = mean + dens[0, l // 2, l % 2, c]
        rho[l : l + 1, :] = jnp.full((1, 128), mean * 0.125, f32)
    rho[4:8, :] = jnp.ones((4, 128), f32)

    prolong_in.wait()
    for h in range(2):
        for s in range(8):
            wide[pl.ds(s * 32, 32), h * 64 : h * 64 + 64] = prolong[
                s, pl.ds(h, 32, stride=2), :
            ]
    w_hi, w_lo = split(wide[...].T)
    w_both = jnp.concatenate([w_hi, w_lo], axis=0)
    row, col = iota((256, 256), 0), iota((256, 256), 1)
    same_pair = lax.rem(row, 32) == col // 8
    cell = lax.rem(iota((1, 256), 1), 8)
    slots_in.wait()
    fine_in.wait()
    ys = []
    for l in range(4):
        slot_of = jnp.zeros((1, 256), jnp.int32)
        for c in range(8):
            slot_of = jnp.where(cell == c, slots[0, l // 2, l % 2, c], slot_of)
        pick = jnp.where(same_pair & (row // 32 == slot_of), 1.0, 0.0).astype(bf16)
        ordered = mm(pick, fine[l]).astype(bf16)
        both = mm(w_both, ordered)
        ys.append(both[:128] + both[128:])
    coarse = []
    for m in range(2):
        y0, y1 = ys[2 * m], ys[2 * m + 1]
        coarse.append(
            jnp.where(left, y0[:64], y1[64:]) + roll(jnp.where(left, y1[:64], y0[64:]), 64)
        )
    r128, l128 = iota((128, 128), 0), iota((128, 128), 1)
    order = jnp.where(
        lax.rem(r128 // q, 2) * 64 + (r128 // rows) * q + lax.rem(r128, q) == l128, 1.0, 0.0
    ).astype(bf16)
    hi, lo = split(jnp.concatenate(coarse, axis=0))
    cut = mm(order, hi, across=1) + mm(order, lo, across=1)
    for chunk in range(chunks):
        pack[chunk, :rows, :] = cut[chunk * rows : chunk * rows + rows]

    stiff_in.wait()
    penalty_in.wait()
    eye = iota((64, 64), 0) == iota((64, 64), 1)
    lane64 = iota((64, 128), 1)
    diags = jnp.zeros((64, 128), f32)
    for s in range(24):
        if s < 8:
            p = prolong[s]
            kp = mm(stiff[...], p, highest)
            matrix = mm(p.T, kp, highest)
            templ[s] = matrix
        else:
            matrix = penalty[s - 8]
        column = jnp.sum(jnp.where(eye, matrix, 0.0), axis=1, keepdims=True)
        diags = jnp.where(lane64 == s, column, diags)
        hi, lo = split(matrix)
        two = jnp.concatenate([hi, lo], axis=1)
        for i in range(2):
            ops[i, s * 32 : s * 32 + 32, 0:128] = two[i * 32 : i * 32 + 32]
            ops[i, s * 32 : s * 32 + 32, 128:192] = hi[i * 32 : i * 32 + 32]

    pl.semaphore_wait(barrier, chunks - 1 + 2 + near - 1 + 1 + 1)

    def rho_copy(i, to_a, to_b):
        return pltpu.make_async_remote_copy(
            src_ref=rho,
            dst_ref=rho_in.at[i],
            send_sem=rho_ss.at[i],
            recv_sem=rho_rs.at[i],
            device_id=(to_a, to_b),
            device_id_type=MESH,
        )

    rho_copies = [
        rho_copy(DOWN_A, up_a, b),
        rho_copy(UP_A, down_a, b),
        rho_copy(DOWN_B, a, up_b),
        rho_copy(UP_B, a, down_b),
    ]
    for copy in rho_copies:
        copy.start()

    neigh_in.wait()
    codes_in.wait()
    for copy in rho_copies:
        copy.wait()
    lane, half = iota((rows, 128), 1), iota((rows, 128), 0) // q
    tile = jnp.ones((rows, 128), f32)
    face_w = []
    for m in range(2):
        for k in range(2):
            l = 2 * m + k
            own = rho[l : l + 1, :]
            faces = {
                DOWN_A: rho_in[DOWN_A, l : l + 1, :],
                UP_A: rho_in[UP_A, l : l + 1, :],
                DOWN_B: rho_in[DOWN_B, 2 + k : 3 + k, :] if m == 0 else rho[k : k + 1, :],
                UP_B: rho[2 + k : 3 + k, :] if m == 0 else rho_in[UP_B, k : k + 1, :],
                (UP_C if k == 0 else DOWN_C): rho[2 * m + 1 - k : 2 * m + 2 - k, :],
            }
            for c in range(8):
                at = (half == k) & (lane == m * 64 + slots[0, m, k, c])
                tile = jnp.where(at, dens[0, m, k, c], tile)
            face_w.append({})
            for face, other in faces.items():
                present = (neigh[0, m, k, face] >= 0).astype(f32)
                face_w[l][face] = 2.0 / (own + other) * present
    tile = 1.0 / tile
    for m in range(2):
        for k in range(2):
            for face in range(6):
                code = codes[0, m, k, face].astype(f32)
                weight = face_w[2 * m + k].get(face, jnp.zeros((1, 128), f32))
                tile = jnp.where((half == k) & (lane == m * 64 + 8 + face), code, tile)
                tile = jnp.where((half == k) & (lane == m * 64 + 14 + face), weight, tile)
    for chunk in range(chunks):
        pack[chunk, rows:, :] = tile

    def held_copy(d):
        chunk, where = device(d)
        return pltpu.make_async_remote_copy(
            src_ref=pack.at[chunk],
            dst_ref=held.at[core, a],
            send_sem=held_ss.at[d],
            recv_sem=held_rs.at[d],
            device_id=where,
            device_id_type=MESH,
        )

    for d in range(1, chunks):
        held_copy(d).start()
    held[core, a] = pack[mine]

    top = jnp.zeros((1, 1), f32)
    for m in range(2):
        for k in range(2):
            diag = jnp.zeros((64, 64), f32)
            for c in range(8):
                weight = 1.0 / jnp.full((1, 64), dens[0, m, k, c], f32)
                diag = diag + weight * templ[slots[0, m, k, c]]
            extent = jnp.zeros((64, 64), f32)
            for face, weight in face_w[2 * m + k].items():
                block = weight[:, :64] * penalty[codes[0, m, k, face]]
                diag = diag + block
                extent = extent + jnp.abs(block)
            jac = jnp.sum(jnp.where(eye, diag, 0.0), axis=1, keepdims=True)
            sums = jnp.sum(jnp.abs(diag) + extent, axis=1, keepdims=True)
            top = jnp.maximum(top, jnp.max(sums / jac, axis=0, keepdims=True))

    top_1[0] = jnp.broadcast_to(top, (8, 128))

    def top1_copy(d):
        return pltpu.make_async_remote_copy(
            src_ref=top_1.at[0],
            dst_ref=top_1.at[d],
            send_sem=top1_ss.at[d],
            recv_sem=top1_rs.at[d],
            device_id=device(d)[1],
            device_id_type=MESH,
        )

    def top2_copy(d):
        return pltpu.make_async_remote_copy(
            src_ref=top_2.at[0],
            dst_ref=top_2.at[d],
            send_sem=top2_ss.at[d],
            recv_sem=top2_rs.at[d],
            device_id=around(d),
            device_id_type=MESH,
        )

    each(1, chunks, lambda d: top1_copy(d).start())

    code16 = iota((16, 128), 0).astype(f32)

    def unpack(j, _):
        got = held[j - 2 * REACH]
        x = got[:, :rows, :].reshape(64, 128).T
        x = jnp.concatenate([x[:64], x[64:]], axis=1)
        meta = got[:, rows:, :].reshape(64, 128).T
        meta = jnp.concatenate([meta[0:32], meta[64:96]], axis=1)
        weights[j] = meta[0:24]
        summed = jnp.zeros((16, 128), f32)
        for face in range(6):
            summed = summed + jnp.where(
                code16 == meta[8 + face : 9 + face], meta[14 + face : 15 + face], 0.0
            )
        table = jnp.concatenate([meta[0:8], summed, jnp.zeros((104, 128), f32)], axis=0)
        over = 1.0 / mm(diags, table, highest)
        rhs[j] = x
        ijac[j] = over
        start[j] = x * over
        vec[j] = x * over
        return 0

    def products(t, which=None):
        def two(i, _):
            j = t // 2 + 2 * i
            hi, lo = split(jnp.concatenate([vec[j], vec[j + 1]], axis=1))
            stack = jnp.concatenate([hi, hi, lo], axis=0)
            for n in range(2):
                every = mm(ops[n], stack)
                at = slice(n * 32, n * 32 + 32)
                for u in range(2):
                    y = every[:, u * 128 : u * 128 + 128]
                    w = weights.at[j + u]
                    result = w[0:1, :] * y[0:32]
                    for s in range(1, 8):
                        result = result + w[s : s + 1, :] * y[s * 32 : s * 32 + 32]
                    g = []
                    for face in range(6):
                        code = jnp.broadcast_to(w[8 + face : 9 + face, :], (32, 128))
                        flux = y[256:288]
                        for c in range(1, 16):
                            flux = jnp.where(code == c, y[256 + c * 32 : 288 + c * 32], flux)
                        g.append(w[14 + face : 15 + face, :] * flux)
                        result = result + g[face]
                    result = result - roll(g[UP_A], rows) - roll(g[DOWN_A], -rows)
                    part[j + u, at, :] = result - roll(g[UP_C], q) - roll(g[DOWN_C], -q)
                    g_up[j + u, at, :] = g[UP_B]
                    g_down[j + u, at, :] = g[DOWN_B]
            return 0

        if which is None:
            lax.fori_loop(0, UNITS // 2 - t // 2, two, 0)
        else:
            lax.fori_loop(0, len(which), lambda i, _: two(which[0] + (which[-1] - which[0]) * i, 0), 0)

    def applied(t, use):
        def one(j, _):
            below, above = max(j - 1, 0), min(j + 1, UNITS - 1)
            low = roll(jnp.where(left, g_up[j], g_up[below]), 64)
            high = roll(jnp.where(left, g_down[above], g_down[j]), 64)
            use(j, part[j] - low - high)
            return 0

        for j in range((t + 1) // 2, UNITS - (t + 1) // 2):
            one(j, 0)

    def keep_first(j, value):
        w0[j] = value
        vec[j] = value * ijac[j]

    each(1, chunks, lambda d: held_copy(d).wait())
    for j in range(2 * REACH, 2 * REACH + 2):
        unpack(j, 0)

    def base_copy(n, ref, side, d):
        return pltpu.make_async_remote_copy(
            src_ref=ref.at[2:4],
            dst_ref=ref.at[4 * side : 4 * side + 2],
            send_sem=base_ss.at[n, side],
            recv_sem=base_rs.at[n, side],
            device_id=along(d),
            device_id_type=MESH,
        )

    base_copies = [base_copy(0, base, 0, 1), base_copy(0, base, 1, pairs - 1)]
    more_copies = [base_copy(1, more, 0, 1), base_copy(1, more, 1, pairs - 1)]
    for copy in base_copies + more_copies:
        copy.start()
    products(0, (REACH,))
    each(1, chunks, lambda d: top1_copy(d).wait())
    top_2[0] = jnp.max(top_1[...], axis=0)
    each(1, near, lambda d: top2_copy(d).start())
    for copy in base_copies:
        copy.wait()
    for j in (0, 1, 4, 5):
        vec[j] = start[j]
    products(0, (0, 2 * REACH))
    for copy in more_copies:
        copy.wait()
    applied(0, keep_first)
    each(1, near, lambda d: top2_copy(d).wait())
    top_3[0] = jnp.max(top_2[...], axis=0)
    top3_copy = pltpu.make_async_remote_copy(
        src_ref=top_3.at[0],
        dst_ref=top_3.at[1],
        send_sem=top3_sems.at[0],
        recv_sem=top3_sems.at[1],
        device_id=opposite,
        device_id_type=MESH,
    )
    top3_copy.start()
    products(1)
    top3_copy.wait()
    upper = jnp.max(top_3[...], axis=0)[0:1, :]

    lower = upper / 10.0
    centre_val = 0.5 * (upper + lower)
    half_width = 0.5 * (upper - lower)
    sigma = centre_val / half_width
    over_centre = 1.0 / centre_val
    damp0 = 1.0 / sigma
    damp1 = 1.0 / (2.0 * sigma - damp0)
    keep1, gain1 = damp1 * damp0, 2.0 * damp1 / half_width
    damp2 = 1.0 / (2.0 * sigma - damp1)
    keep2, gain2 = damp2 * damp1, 2.0 * damp2 / half_width

    def combine(j, second):
        over, first = ijac[j], w0[j]
        update0 = rhs[j] * over * over_centre
        resid1 = rhs[j] - first * over_centre
        update1 = keep1 * update0 + gain1 * (resid1 * over)
        both = (keep1 * over_centre) * first + gain1 * (first - over_centre * second)
        resid2 = resid1 - both
        update2 = keep2 * update1 + gain2 * (resid2 * over)
        resid[j] = resid2
        total[j] = update0 + update1 + update2
        vec[j] = update2

    applied(1, combine)

    def sweep(t, damp, multiply=products):
        damp_next = 1.0 / (2.0 * sigma - damp)
        keep, gain = damp_next * damp, 2.0 * damp_next / half_width

        def step(j, value):
            now = resid[j] - value
            resid[j] = now
            update = keep * vec[j] + gain * (now * ijac[j])
            total[j] = total[j] + update
            vec[j] = update

        multiply(t)
        applied(t, step)
        return damp_next

    damp = damp2
    for t in range(2, SPAN):
        damp = sweep(t, damp)

    edge[0] = vec[2 * REACH : 2 * REACH + 2]
    edge[1] = resid[2 * REACH : 2 * REACH + 2]

    def edge_copy(n, side, d):
        return pltpu.make_async_remote_copy(
            src_ref=edge.at[n],
            dst_ref=edge_in.at[side, n],
            send_sem=edge_ss.at[n, side],
            recv_sem=edge_rs.at[n, side],
            device_id=along(d),
            device_id_type=MESH,
        )

    vec_copies, resid_copies = [
        [edge_copy(n, 0, 1), edge_copy(n, 1, pairs - 1)] for n in range(2)
    ]
    for copy in vec_copies + resid_copies:
        copy.start()
    products(0, (REACH,))
    for copy in vec_copies:
        copy.wait()
    for side in range(2):
        vec[4 * side : 4 * side + 2] = edge_in[side, 0]

    def outer(t):
        products(t, (0, 2 * REACH))
        for copy in resid_copies:
            copy.wait()
        for side in range(2):
            resid[4 * side : 4 * side + 2] = edge_in[side, 1]

    damp = sweep(0, damp, outer)
    for t in range(1, SWEEPS - SPAN):
        damp = sweep(t, damp)

    for u in range(2):
        x = total[2 * REACH + u]
        done[u] = jnp.concatenate([x[:, :64], x[:, 64:]], axis=0).T

    def parts_copy(d):
        chunk, where = device(d)
        return pltpu.make_async_remote_copy(
            src_ref=done.at[lax.rem(chunk, 2)],
            dst_ref=parts.at[mine],
            send_sem=parts_ss.at[d],
            recv_sem=parts_rs.at[d],
            device_id=where,
            device_id_type=MESH,
        )

    each(1, chunks, lambda d: parts_copy(d).start())
    parts[mine] = done[core]
    each(1, chunks, lambda d: parts_copy(d).wait())

    even = lax.rem(iota((64, 128), 0), 2) == 0

    def out_copy(i):
        return pltpu.make_async_copy(ready.at[i], out.at[i], out_sems.at[i])

    def place(i, _):
        at = pl.ds(i * rows, rows)
        hi, lo = split(parts[:, at, :].reshape(128, 128).T)
        x = mm(hi, order) + mm(lo, order)
        for m in range(2):
            own = x[m * 64 : m * 64 + 64]
            turned = roll(own, 64)
            moved = jnp.where(even, pltpu.roll(turned, 63, 0), pltpu.roll(turned, 1, 0))
            ready[i, m] = jnp.where(even == left, own, moved)
        out_copy(i).start()
        return 0

    for i in range(slabs):
        place(i, 0)
    each(0, slabs, lambda i: out_copy(i).wait())


def local(slabs, grps, dens, slots, neigh, codes, stiff, prolong, penalty, fine):
    x = fine.reshape(4, 8, 32, 128).transpose(0, 2, 1, 3).reshape(4, 256, 128)
    smem, vmem = pltpu.SMEM, pltpu.VMEM
    args = (dens, slots, neigh, codes, stiff, prolong, penalty, x)
    dma = pltpu.SemaphoreType.DMA
    chunks, pairs = 2 * slabs, grps // 2
    rows = 128 // chunks
    columns = pltpu.VMEM((UNITS, 64, 128), f32)
    result = pl.pallas_call(
        functools.partial(kernel, slabs, grps),
        out_shape=jax.ShapeDtypeStruct((slabs, 2, 64, 128), f32),
        in_specs=[pl.BlockSpec(memory_space=pl.ANY)] * 8,
        out_specs=pl.BlockSpec(memory_space=pl.ANY),
        scratch_shapes=[
            *(space(v.shape, v.dtype) for space, v in zip([smem] * 4 + [vmem] * 4, args)),
            dma((8,)),
            pltpu.VMEM((8, 128), f32),
            pltpu.VMEM((4, 8, 128), f32),
            pltpu.VMEM((8, 64, 64), f32),
            pltpu.VMEM((256, 128), f32),
            pltpu.VMEM((2, 768, 192), bf16),
            pltpu.VMEM((chunks, 2 * rows, 128), f32),
            pltpu.VMEM((2, slabs, 2 * rows, 128), f32),
            pltpu.VMEM((UNITS, 88, 128), f32),
            pltpu.VMEM((UNITS, 128, 128), f32),
            *[columns] * 7,
            pltpu.VMEM((chunks, 8, 128), f32),
            pltpu.VMEM((pairs // 2, 8, 128), f32),
            pltpu.VMEM((2, 8, 128), f32),
            pltpu.VMEM((2, 2, 64, 128), f32),
            pltpu.VMEM((2, 2, 2, 64, 128), f32),
            pltpu.VMEM((2, 64, 128), f32),
            pltpu.VMEM((chunks, 64, 128), f32),
            pltpu.VMEM((slabs, 2, 64, 128), f32),
            dma((slabs,)),
            dma((4,)),
            dma((4,)),
            dma((chunks,)),
            dma((chunks,)),
            dma((chunks,)),
            dma((chunks,)),
            dma((pairs // 2,)),
            dma((pairs // 2,)),
            dma((2,)),
            dma((2, 2)),
            dma((2, 2)),
            dma((2, 2)),
            dma((2, 2)),
            dma((chunks,)),
            dma((chunks,)),
        ],
        compiler_params=pltpu.CompilerParams(collective_id=0, has_side_effects=True),
    )(*args)
    spread = result.reshape(slabs, 2, 32, 2, 128).transpose(0, 1, 3, 2, 4)
    return spread.reshape(slabs, 2, 2, 4096)


def solution(mesh):
    return jax.shard_map(
        functools.partial(local, mesh.shape["slab"], mesh.shape["grp"]),
        mesh=mesh,
        in_specs=(
            P("slab", "grp", None, None),
            P("slab", "grp", None, None),
            P("slab", "grp", None, None),
            P("slab", "grp", None, None),
            P(),
            P(),
            P(),
            P("slab", "grp", None, None, None),
        ),
        out_specs=P(None, "grp", None, None),
        check_vma=False,
    )
```

```python
import functools

import jax
import jax.numpy as jnp
from jax import lax
from jax.experimental import pallas as pl
from jax.experimental.pallas import tpu as pltpu
from jax.sharding import PartitionSpec as P

SWEEPS = 8
REACH = 1
SPAN = 4 * REACH
UNITS = 4 * REACH + 2

MESH = pl.DeviceIdType.MESH
f32, bf16 = jnp.float32, jnp.bfloat16
highest = lax.Precision.HIGHEST
DOWN_A, UP_A, DOWN_B, UP_B, DOWN_C, UP_C = range(6)


def split(x):
    hi = x.astype(bf16)
    return hi, (x - hi.astype(f32)).astype(bf16)


def mm(a, b, precision=None, across=0):
    return lax.dot_general(
        a, b, (((1,), (across,)), ((), ())), precision=precision, preferred_element_type=f32
    )


def roll(x, by):
    return pltpu.roll(x, by % 128, 1)


def iota(shape, dim):
    return lax.broadcasted_iota(jnp.int32, shape, dim)


def kernel(
    slabs,
    grps,
    dens_hbm,
    slots_hbm,
    neigh_hbm,
    codes_hbm,
    stiff_hbm,
    prolong_hbm,
    penalty_hbm,
    fine_hbm,
    out,
    dens,
    slots,
    neigh,
    codes,
    stiff,
    prolong,
    penalty,
    fine,
    in_sems,
    rho,
    rho_in,
    templ,
    wide,
    ops,
    pack,
    held,
    base,
    more,
    vec,
    part,
    g_up,
    g_down,
    w0,
    resid,
    total,
    top_1,
    top_2,
    top_3,
    edge,
    edge_in,
    done,
    parts,
    ready,
    out_sems,
    rho_ss,
    rho_rs,
    held_ss,
    held_rs,
    top1_ss,
    top1_rs,
    top2_ss,
    top2_rs,
    top3_sems,
    base_ss,
    base_rs,
    edge_ss,
    edge_rs,
    parts_ss,
    parts_rs,
):
    chunks = 2 * slabs
    q = 64 // chunks
    rows = 2 * q
    pairs = grps // 2
    a = lax.axis_index("slab")
    b = lax.axis_index("grp")
    core = lax.rem(b, 2)
    pair = b // 2
    mine = 2 * a + core
    up_a, down_a = lax.rem(a + 1, slabs), lax.rem(a + slabs - 1, slabs)
    up_b, down_b = lax.rem(b + 1, grps), lax.rem(b + grps - 1, grps)

    loads = [
        pltpu.make_async_copy(src, dst, in_sems.at[i])
        for i, (src, dst) in enumerate(
            (
                (dens_hbm, dens),
                (slots_hbm, slots),
                (neigh_hbm, neigh),
                (codes_hbm, codes),
                (stiff_hbm, stiff),
                (prolong_hbm, prolong),
                (penalty_hbm, penalty),
                (fine_hbm, fine),
            )
        )
    ]
    dens_in, slots_in, neigh_in, codes_in, stiff_in, prolong_in, penalty_in, fine_in = loads
    for load in loads:
        load.start()

    def each(first, last, act):
        def body(d, _):
            act(d)
            return 0

        lax.fori_loop(first, last, body, 0)

    def device(d):
        chunk = lax.rem(mine + d, chunks)
        return chunk, (chunk // 2, 2 * pair + lax.rem(chunk, 2))

    def along(d):
        return (a, 2 * lax.rem(pair + d, pairs) + core)

    near = pairs // 2

    def around(d):
        return (a, 2 * (pair // near * near + lax.rem(lax.rem(pair, near) + d, near)) + core)

    opposite = along(near)
    start, weights = base.at[:, 0:64], base.at[:, 64:88]
    rhs, ijac = more.at[:, 0:64], more.at[:, 64:128]

    barrier = pltpu.get_barrier_semaphore()

    def greet(where):
        pl.semaphore_signal(barrier, inc=1, device_id=where, device_id_type=MESH)

    for d in range(1, chunks):
        greet(device(d)[1])
    greet(along(1))
    greet(along(pairs - 1))
    for d in range(1, near):
        greet(around(d))
    greet(opposite)
    greet((a, lax.rem(b + grps - 1 + 2 * core, grps)))

    left = iota((64, 128), 1) < 64

    dens_in.wait()
    for l in range(4):
        mean = dens[0, l // 2, l % 2, 0]
        for c in range(1, 8):
            mean = mean + dens[0, l // 2, l % 2, c]
        rho[l : l + 1, :] = jnp.full((1, 128), mean * 0.125, f32)
    rho[4:8, :] = jnp.ones((4, 128), f32)

    prolong_in.wait()
    for h in range(2):
        for s in range(8):
            wide[pl.ds(s * 32, 32), h * 64 : h * 64 + 64] = prolong[
                s, pl.ds(h, 32, stride=2), :
            ]
    w_hi, w_lo = split(wide[...].T)
    w_both = jnp.concatenate([w_hi, w_lo], axis=0)
    row, col = iota((256, 256), 0), iota((256, 256), 1)
    same_pair = lax.rem(row, 32) == col // 8
    cell = lax.rem(iota((1, 256), 1), 8)
    slots_in.wait()
    fine_in.wait()
    ys = []
    for l in range(4):
        slot_of = jnp.zeros((1, 256), jnp.int32)
        for c in range(8):
            slot_of = jnp.where(cell == c, slots[0, l // 2, l % 2, c], slot_of)
        pick = jnp.where(same_pair & (row // 32 == slot_of), 1.0, 0.0).astype(bf16)
        ordered = mm(pick, fine[l]).astype(bf16)
        both = mm(w_both, ordered)
        ys.append(both[:128] + both[128:])
    coarse = []
    for m in range(2):
        y0, y1 = ys[2 * m], ys[2 * m + 1]
        coarse.append(
            jnp.where(left, y0[:64], y1[64:]) + roll(jnp.where(left, y1[:64], y0[64:]), 64)
        )
    r128, l128 = iota((128, 128), 0), iota((128, 128), 1)
    order = jnp.where(
        lax.rem(r128 // q, 2) * 64 + (r128 // rows) * q + lax.rem(r128, q) == l128, 1.0, 0.0
    ).astype(bf16)
    hi, lo = split(jnp.concatenate(coarse, axis=0))
    cut = mm(order, hi, across=1) + mm(order, lo, across=1)
    for chunk in range(chunks):
        pack[chunk, :rows, :] = cut[chunk * rows : chunk * rows + rows]

    stiff_in.wait()
    penalty_in.wait()
    eye = iota((64, 64), 0) == iota((64, 64), 1)
    lane64 = iota((64, 128), 1)
    diags = jnp.zeros((64, 128), f32)
    for s in range(24):
        if s < 8:
            p = prolong[s]
            kp = mm(stiff[...], p, highest)
            matrix = mm(p.T, kp, highest)
            templ[s] = matrix
        else:
            matrix = penalty[s - 8]
        column = jnp.sum(jnp.where(eye, matrix, 0.0), axis=1, keepdims=True)
        diags = jnp.where(lane64 == s, column, diags)
        hi, lo = split(matrix)
        two = jnp.concatenate([hi, lo], axis=1)
        for i in range(2):
            ops[i, s * 32 : s * 32 + 32, 0:128] = two[i * 32 : i * 32 + 32]
            ops[i, s * 32 : s * 32 + 32, 128:192] = hi[i * 32 : i * 32 + 32]

    pl.semaphore_wait(barrier, chunks - 1 + 2 + near - 1 + 1 + 1)

    def rho_copy(i, to_a, to_b):
        return pltpu.make_async_remote_copy(
            src_ref=rho,
            dst_ref=rho_in.at[i],
            send_sem=rho_ss.at[i],
            recv_sem=rho_rs.at[i],
            device_id=(to_a, to_b),
            device_id_type=MESH,
        )

    rho_copies = [
        rho_copy(DOWN_A, up_a, b),
        rho_copy(UP_A, down_a, b),
        rho_copy(DOWN_B, a, up_b),
        rho_copy(UP_B, a, down_b),
    ]
    for copy in rho_copies:
        copy.start()

    neigh_in.wait()
    codes_in.wait()
    for copy in rho_copies:
        copy.wait()
    lane, half = iota((rows, 128), 1), iota((rows, 128), 0) // q
    tile = jnp.ones((rows, 128), f32)
    face_w = []
    for m in range(2):
        for k in range(2):
            l = 2 * m + k
            own = rho[l : l + 1, :]
            faces = {
                DOWN_A: rho_in[DOWN_A, l : l + 1, :],
                UP_A: rho_in[UP_A, l : l + 1, :],
                DOWN_B: rho_in[DOWN_B, 2 + k : 3 + k, :] if m == 0 else rho[k : k + 1, :],
                UP_B: rho[2 + k : 3 + k, :] if m == 0 else rho_in[UP_B, k : k + 1, :],
                (UP_C if k == 0 else DOWN_C): rho[2 * m + 1 - k : 2 * m + 2 - k, :],
            }
            for c in range(8):
                at = (half == k) & (lane == m * 64 + slots[0, m, k, c])
                tile = jnp.where(at, dens[0, m, k, c], tile)
            face_w.append({})
            for face, other in faces.items():
                present = (neigh[0, m, k, face] >= 0).astype(f32)
                face_w[l][face] = 2.0 / (own + other) * present
    tile = 1.0 / tile
    for m in range(2):
        for k in range(2):
            for face in range(6):
                code = codes[0, m, k, face].astype(f32)
                weight = face_w[2 * m + k].get(face, jnp.zeros((1, 128), f32))
                tile = jnp.where((half == k) & (lane == m * 64 + 8 + face), code, tile)
                tile = jnp.where((half == k) & (lane == m * 64 + 14 + face), weight, tile)
    for chunk in range(chunks):
        pack[chunk, rows:, :] = tile

    def held_copy(d):
        chunk, where = device(d)
        return pltpu.make_async_remote_copy(
            src_ref=pack.at[chunk],
            dst_ref=held.at[core, a],
            send_sem=held_ss.at[d],
            recv_sem=held_rs.at[d],
            device_id=where,
            device_id_type=MESH,
        )

    for d in range(1, chunks):
        held_copy(d).start()
    held[core, a] = pack[mine]

    top = jnp.zeros((1, 1), f32)
    for m in range(2):
        for k in range(2):
            diag = jnp.zeros((64, 64), f32)
            for c in range(8):
                weight = 1.0 / jnp.full((1, 64), dens[0, m, k, c], f32)
                diag = diag + weight * templ[slots[0, m, k, c]]
            extent = jnp.zeros((64, 64), f32)
            for face, weight in face_w[2 * m + k].items():
                block = weight[:, :64] * penalty[codes[0, m, k, face]]
                diag = diag + block
                extent = extent + jnp.abs(block)
            jac = jnp.sum(jnp.where(eye, diag, 0.0), axis=1, keepdims=True)
            sums = jnp.sum(jnp.abs(diag) + extent, axis=1, keepdims=True)
            top = jnp.maximum(top, jnp.max(sums / jac, axis=0, keepdims=True))

    top_1[0] = jnp.broadcast_to(top, (8, 128))

    def top1_copy(d):
        return pltpu.make_async_remote_copy(
            src_ref=top_1.at[0],
            dst_ref=top_1.at[d],
            send_sem=top1_ss.at[d],
            recv_sem=top1_rs.at[d],
            device_id=device(d)[1],
            device_id_type=MESH,
        )

    def top2_copy(d):
        return pltpu.make_async_remote_copy(
            src_ref=top_2.at[0],
            dst_ref=top_2.at[d],
            send_sem=top2_ss.at[d],
            recv_sem=top2_rs.at[d],
            device_id=around(d),
            device_id_type=MESH,
        )

    each(1, chunks, lambda d: top1_copy(d).start())

    code16 = iota((16, 128), 0).astype(f32)

    def unpack(j, _):
        got = held[j - 2 * REACH]
        x = got[:, :rows, :].reshape(64, 128).T
        x = jnp.concatenate([x[:64], x[64:]], axis=1)
        meta = got[:, rows:, :].reshape(64, 128).T
        meta = jnp.concatenate([meta[0:32], meta[64:96]], axis=1)
        weights[j] = meta[0:24]
        summed = jnp.zeros((16, 128), f32)
        for face in range(6):
            summed = summed + jnp.where(
                code16 == meta[8 + face : 9 + face], meta[14 + face : 15 + face], 0.0
            )
        table = jnp.concatenate([meta[0:8], summed, jnp.zeros((104, 128), f32)], axis=0)
        over = 1.0 / mm(diags, table, highest)
        rhs[j] = x
        ijac[j] = over
        start[j] = x * over
        vec[j] = x * over
        return 0

    own_units = range(2 * REACH, 2 * REACH + 2)

    def products(t, which=None):
        def two(i, _):
            j = t // 2 + 2 * i
            hi, lo = split(jnp.concatenate([vec[j], vec[j + 1]], axis=1))
            stack = jnp.concatenate([hi, hi, lo], axis=0)
            for n in range(2):
                every = mm(ops[n], stack)
                at = slice(n * 32, n * 32 + 32)
                for u in range(2):
                    y = every[:, u * 128 : u * 128 + 128]
                    w = weights.at[j + u]

                    def flux_of(face):
                        code = jnp.broadcast_to(w[8 + face : 9 + face, :], (32, 128))
                        flux = y[256:288]
                        for c in range(1, 16):
                            flux = jnp.where(code == c, y[256 + c * 32 : 288 + c * 32], flux)
                        return w[14 + face : 15 + face, :] * flux

                    if j + u < (t + 1) // 2:
                        g_up[j + u, at, :] = flux_of(UP_B)
                        continue
                    if j + u >= UNITS - (t + 1) // 2:
                        g_down[j + u, at, :] = flux_of(DOWN_B)
                        continue
                    result = w[0:1, :] * y[0:32]
                    for s in range(1, 8):
                        result = result + w[s : s + 1, :] * y[s * 32 : s * 32 + 32]
                    g = []
                    for face in range(6):
                        g.append(flux_of(face))
                        result = result + g[face]
                    result = result - roll(g[UP_A], rows) - roll(g[DOWN_A], -rows)
                    part[j + u, at, :] = result - roll(g[UP_C], q) - roll(g[DOWN_C], -q)
                    g_up[j + u, at, :] = g[UP_B]
                    g_down[j + u, at, :] = g[DOWN_B]
            return 0

        for i in range(UNITS // 2 - t // 2) if which is None else which:
            two(i, 0)

    def applied(t, use):
        def one(j, _):
            below, above = max(j - 1, 0), min(j + 1, UNITS - 1)
            low = roll(jnp.where(left, g_up[j], g_up[below]), 64)
            high = roll(jnp.where(left, g_down[above], g_down[j]), 64)
            use(j, part[j] - low - high)
            return 0

        for j in range((t + 1) // 2, UNITS - (t + 1) // 2):
            one(j, 0)

    def keep_first(j, value):
        w0[j] = value
        vec[j] = value * ijac[j]

    each(1, chunks, lambda d: held_copy(d).wait())
    for j in range(2 * REACH, 2 * REACH + 2):
        unpack(j, 0)

    def base_copy(n, ref, side, d):
        return pltpu.make_async_remote_copy(
            src_ref=ref.at[2:4],
            dst_ref=ref.at[4 * side : 4 * side + 2],
            send_sem=base_ss.at[n, side],
            recv_sem=base_rs.at[n, side],
            device_id=along(d),
            device_id_type=MESH,
        )

    base_copies = [base_copy(0, base, 0, 1), base_copy(0, base, 1, pairs - 1)]
    more_copies = [base_copy(1, more, 0, 1), base_copy(1, more, 1, pairs - 1)]
    for copy in base_copies + more_copies:
        copy.start()
    products(0, (REACH,))
    each(1, chunks, lambda d: top1_copy(d).wait())
    top_2[0] = jnp.max(top_1[...], axis=0)
    each(1, near, lambda d: top2_copy(d).start())
    for copy in base_copies:
        copy.wait()
    for j in (0, 1, 4, 5):
        vec[j] = start[j]
    products(0, (0, 2 * REACH))
    for copy in more_copies:
        copy.wait()
    applied(0, keep_first)
    each(1, near, lambda d: top2_copy(d).wait())
    top_3[0] = jnp.max(top_2[...], axis=0)
    top3_copy = pltpu.make_async_remote_copy(
        src_ref=top_3.at[0],
        dst_ref=top_3.at[1],
        send_sem=top3_sems.at[0],
        recv_sem=top3_sems.at[1],
        device_id=opposite,
        device_id_type=MESH,
    )
    top3_copy.start()
    products(1)
    top3_copy.wait()
    upper = jnp.max(top_3[...], axis=0)[0:1, :]

    lower = upper / 10.0
    centre_val = 0.5 * (upper + lower)
    half_width = 0.5 * (upper - lower)
    sigma = centre_val / half_width
    over_centre = 1.0 / centre_val
    damp0 = 1.0 / sigma
    damp1 = 1.0 / (2.0 * sigma - damp0)
    keep1, gain1 = damp1 * damp0, 2.0 * damp1 / half_width
    damp2 = 1.0 / (2.0 * sigma - damp1)
    keep2, gain2 = damp2 * damp1, 2.0 * damp2 / half_width

    def combine(j, second):
        over, first = ijac[j], w0[j]
        update0 = rhs[j] * over * over_centre
        resid1 = rhs[j] - first * over_centre
        update1 = keep1 * update0 + gain1 * (resid1 * over)
        both = (keep1 * over_centre) * first + gain1 * (first - over_centre * second)
        resid2 = resid1 - both
        update2 = keep2 * update1 + gain2 * (resid2 * over)
        resid[j] = resid2
        if j in own_units:
            total[j - 2 * REACH] = update0 + update1 + update2
        vec[j] = update2

    applied(1, combine)

    def sweep(t, damp, multiply=products):
        damp_next = 1.0 / (2.0 * sigma - damp)
        keep, gain = damp_next * damp, 2.0 * damp_next / half_width

        def step(j, value):
            now = resid[j] - value
            resid[j] = now
            update = keep * vec[j] + gain * (now * ijac[j])
            if j in own_units:
                total[j - 2 * REACH] = total[j - 2 * REACH] + update
            vec[j] = update

        multiply(t)
        applied(t, step)
        return damp_next

    damp = damp2
    for t in range(2, SPAN):
        damp = sweep(t, damp)

    edge[0] = vec[2 * REACH : 2 * REACH + 2]
    edge[1] = resid[2 * REACH : 2 * REACH + 2]

    def edge_copy(n, side, d):
        return pltpu.make_async_remote_copy(
            src_ref=edge.at[n],
            dst_ref=edge_in.at[side, n],
            send_sem=edge_ss.at[n, side],
            recv_sem=edge_rs.at[n, side],
            device_id=along(d),
            device_id_type=MESH,
        )

    vec_copies, resid_copies = [
        [edge_copy(n, 0, 1), edge_copy(n, 1, pairs - 1)] for n in range(2)
    ]
    for copy in vec_copies + resid_copies:
        copy.start()
    products(0, (REACH,))
    for copy in vec_copies:
        copy.wait()
    for side in range(2):
        vec[4 * side : 4 * side + 2] = edge_in[side, 0]

    def outer(t):
        products(t, (0, 2 * REACH))
        for copy in resid_copies:
            copy.wait()
        for side in range(2):
            resid[4 * side : 4 * side + 2] = edge_in[side, 1]

    damp = sweep(0, damp, outer)
    for t in range(1, SWEEPS - SPAN):
        damp = sweep(t, damp)

    for u in range(2):
        x = total[u]
        done[u] = jnp.concatenate([x[:, :64], x[:, 64:]], axis=0).T

    def parts_copy(d):
        chunk, where = device(d)
        return pltpu.make_async_remote_copy(
            src_ref=done.at[lax.rem(chunk, 2)],
            dst_ref=parts.at[mine],
            send_sem=parts_ss.at[d],
            recv_sem=parts_rs.at[d],
            device_id=where,
            device_id_type=MESH,
        )

    each(1, chunks, lambda d: parts_copy(d).start())
    parts[mine] = done[core]
    each(1, chunks, lambda d: parts_copy(d).wait())

    even = lax.rem(iota((64, 128), 0), 2) == 0

    def out_copy(i):
        return pltpu.make_async_copy(ready.at[i], out.at[i], out_sems.at[i])

    def place(i, _):
        at = pl.ds(i * rows, rows)
        hi, lo = split(parts[:, at, :].reshape(128, 128).T)
        x = mm(hi, order) + mm(lo, order)
        for m in range(2):
            own = x[m * 64 : m * 64 + 64]
            turned = roll(own, 64)
            moved = jnp.where(even, pltpu.roll(turned, 63, 0), pltpu.roll(turned, 1, 0))
            ready[i, m] = jnp.where(even == left, own, moved)
        out_copy(i).start()
        return 0

    for i in range(slabs):
        place(i, 0)
    each(0, slabs, lambda i: out_copy(i).wait())


def local(slabs, grps, dens, slots, neigh, codes, stiff, prolong, penalty, fine):
    x = fine.reshape(4, 8, 32, 128).transpose(0, 2, 1, 3).reshape(4, 256, 128)
    smem, vmem = pltpu.SMEM, pltpu.VMEM
    args = (dens, slots, neigh, codes, stiff, prolong, penalty, x)
    dma = pltpu.SemaphoreType.DMA
    chunks, pairs = 2 * slabs, grps // 2
    rows = 128 // chunks
    columns = pltpu.VMEM((UNITS, 64, 128), f32)
    result = pl.pallas_call(
        functools.partial(kernel, slabs, grps),
        out_shape=jax.ShapeDtypeStruct((slabs, 2, 64, 128), f32),
        in_specs=[pl.BlockSpec(memory_space=pl.ANY)] * 8,
        out_specs=pl.BlockSpec(memory_space=pl.ANY),
        scratch_shapes=[
            *(space(v.shape, v.dtype) for space, v in zip([smem] * 4 + [vmem] * 4, args)),
            dma((8,)),
            pltpu.VMEM((8, 128), f32),
            pltpu.VMEM((4, 8, 128), f32),
            pltpu.VMEM((8, 64, 64), f32),
            pltpu.VMEM((256, 128), f32),
            pltpu.VMEM((2, 768, 192), bf16),
            pltpu.VMEM((chunks, 2 * rows, 128), f32),
            pltpu.VMEM((2, slabs, 2 * rows, 128), f32),
            pltpu.VMEM((UNITS, 88, 128), f32),
            pltpu.VMEM((UNITS, 128, 128), f32),
            *[columns] * 6,
            pltpu.VMEM((2, 64, 128), f32),
            pltpu.VMEM((chunks, 8, 128), f32),
            pltpu.VMEM((pairs // 2, 8, 128), f32),
            pltpu.VMEM((2, 8, 128), f32),
            pltpu.VMEM((2, 2, 64, 128), f32),
            pltpu.VMEM((2, 2, 2, 64, 128), f32),
            pltpu.VMEM((2, 64, 128), f32),
            pltpu.VMEM((chunks, 64, 128), f32),
            pltpu.VMEM((slabs, 2, 64, 128), f32),
            dma((slabs,)),
            dma((4,)),
            dma((4,)),
            dma((chunks,)),
            dma((chunks,)),
            dma((chunks,)),
            dma((chunks,)),
            dma((pairs // 2,)),
            dma((pairs // 2,)),
            dma((2,)),
            dma((2, 2)),
            dma((2, 2)),
            dma((2, 2)),
            dma((2, 2)),
            dma((chunks,)),
            dma((chunks,)),
        ],
        compiler_params=pltpu.CompilerParams(collective_id=0, has_side_effects=True),
    )(*args)
    spread = result.reshape(slabs, 2, 32, 2, 128).transpose(0, 1, 3, 2, 4)
    return spread.reshape(slabs, 2, 2, 4096)


def solution(mesh):
    return jax.shard_map(
        functools.partial(local, mesh.shape["slab"], mesh.shape["grp"]),
        mesh=mesh,
        in_specs=(
            P("slab", "grp", None, None),
            P("slab", "grp", None, None),
            P("slab", "grp", None, None),
            P("slab", "grp", None, None),
            P(),
            P(),
            P(),
            P("slab", "grp", None, None, None),
        ),
        out_specs=P(None, "grp", None, None),
        check_vma=False,
    )
```

```python
import functools

import jax
import jax.numpy as jnp
from jax import lax
from jax.experimental import pallas as pl
from jax.experimental.pallas import tpu as pltpu
from jax.sharding import PartitionSpec as P

SWEEPS = 8
REACH = 1
SPAN = 4 * REACH
UNITS = 4 * REACH + 2

MESH = pl.DeviceIdType.MESH
f32, bf16 = jnp.float32, jnp.bfloat16
highest = lax.Precision.HIGHEST
DOWN_A, UP_A, DOWN_B, UP_B, DOWN_C, UP_C = range(6)


def split(x):
    hi = x.astype(bf16)
    return hi, (x - hi.astype(f32)).astype(bf16)


def mm(a, b, precision=None, across=0):
    return lax.dot_general(
        a, b, (((1,), (across,)), ((), ())), precision=precision, preferred_element_type=f32
    )


def roll(x, by):
    return pltpu.roll(x, by % 128, 1)


def iota(shape, dim):
    return lax.broadcasted_iota(jnp.int32, shape, dim)


def kernel(
    slabs,
    grps,
    dens_hbm,
    slots_hbm,
    neigh_hbm,
    codes_hbm,
    stiff_hbm,
    prolong_hbm,
    penalty_hbm,
    fine_hbm,
    out,
    dens,
    slots,
    neigh,
    codes,
    stiff,
    prolong,
    penalty,
    fine,
    in_sems,
    rho,
    rho_in,
    templ,
    wide,
    ops,
    pack,
    held,
    base,
    more,
    vec,
    part,
    g_up,
    g_down,
    w0,
    resid,
    total,
    top_1,
    top_2,
    top_3,
    edge,
    edge_in,
    done,
    parts,
    ready,
    out_sems,
    rho_ss,
    rho_rs,
    held_ss,
    held_rs,
    top1_ss,
    top1_rs,
    top2_ss,
    top2_rs,
    top3_sems,
    base_ss,
    base_rs,
    edge_ss,
    edge_rs,
    parts_ss,
    parts_rs,
):
    chunks = 2 * slabs
    q = 64 // chunks
    rows = 2 * q
    pairs = grps // 2
    a = lax.axis_index("slab")
    b = lax.axis_index("grp")
    core = lax.rem(b, 2)
    pair = b // 2
    mine = 2 * a + core
    up_a, down_a = lax.rem(a + 1, slabs), lax.rem(a + slabs - 1, slabs)
    up_b, down_b = lax.rem(b + 1, grps), lax.rem(b + grps - 1, grps)

    loads = [
        pltpu.make_async_copy(src, dst, in_sems.at[i])
        for i, (src, dst) in enumerate(
            (
                (dens_hbm, dens),
                (slots_hbm, slots),
                (neigh_hbm, neigh),
                (codes_hbm, codes),
                (stiff_hbm, stiff),
                (prolong_hbm, prolong),
                (penalty_hbm, penalty),
                (fine_hbm, fine),
            )
        )
    ]
    dens_in, slots_in, neigh_in, codes_in, stiff_in, prolong_in, penalty_in, fine_in = loads
    for load in loads:
        load.start()

    def each(first, last, act):
        def body(d, _):
            act(d)
            return 0

        lax.fori_loop(first, last, body, 0)

    ring = slabs // 2
    far_first = sorted(
        range(1, chunks),
        key=lambda d: -min(d // 2 % ring, ring - d // 2 % ring) - (d // 2 >= ring),
    )

    def device(d):
        chunk = lax.rem(mine + d, chunks)
        return chunk, (chunk // 2, 2 * pair + lax.rem(chunk, 2))

    def along(d):
        return (a, 2 * lax.rem(pair + d, pairs) + core)

    near = pairs // 2

    def around(d):
        return (a, 2 * (pair // near * near + lax.rem(lax.rem(pair, near) + d, near)) + core)

    opposite = along(near)
    start, weights = base.at[:, 0:64], base.at[:, 64:88]
    rhs, ijac = more.at[:, 0:64], more.at[:, 64:128]

    barrier = pltpu.get_barrier_semaphore()

    def greet(where):
        pl.semaphore_signal(barrier, inc=1, device_id=where, device_id_type=MESH)

    for d in range(1, chunks):
        greet(device(d)[1])
    greet(along(1))
    greet(along(pairs - 1))
    for d in range(1, near):
        greet(around(d))
    greet(opposite)
    greet((a, lax.rem(b + grps - 1 + 2 * core, grps)))

    left = iota((64, 128), 1) < 64

    dens_in.wait()
    for l in range(4):
        mean = dens[0, l // 2, l % 2, 0]
        for c in range(1, 8):
            mean = mean + dens[0, l // 2, l % 2, c]
        rho[l : l + 1, :] = jnp.full((1, 128), mean * 0.125, f32)
    rho[4:8, :] = jnp.ones((4, 128), f32)

    prolong_in.wait()
    for h in range(2):
        for s in range(8):
            wide[pl.ds(s * 32, 32), h * 64 : h * 64 + 64] = prolong[
                s, pl.ds(h, 32, stride=2), :
            ]
    w_hi, w_lo = split(wide[...].T)
    w_both = jnp.concatenate([w_hi, w_lo], axis=0)
    row, col = iota((256, 256), 0), iota((256, 256), 1)
    same_pair = lax.rem(row, 32) == col // 8
    cell = lax.rem(iota((1, 256), 1), 8)
    slots_in.wait()
    fine_in.wait()
    ys = []
    for l in range(4):
        slot_of = jnp.zeros((1, 256), jnp.int32)
        for c in range(8):
            slot_of = jnp.where(cell == c, slots[0, l // 2, l % 2, c], slot_of)
        pick = jnp.where(same_pair & (row // 32 == slot_of), 1.0, 0.0).astype(bf16)
        ordered = mm(pick, fine[l]).astype(bf16)
        both = mm(w_both, ordered)
        ys.append(both[:128] + both[128:])
    coarse = []
    for m in range(2):
        y0, y1 = ys[2 * m], ys[2 * m + 1]
        coarse.append(
            jnp.where(left, y0[:64], y1[64:]) + roll(jnp.where(left, y1[:64], y0[64:]), 64)
        )
    r128, l128 = iota((128, 128), 0), iota((128, 128), 1)
    order = jnp.where(
        lax.rem(r128 // q, 2) * 64 + (r128 // rows) * q + lax.rem(r128, q) == l128, 1.0, 0.0
    ).astype(bf16)
    hi, lo = split(jnp.concatenate(coarse, axis=0))
    cut = mm(order, hi, across=1) + mm(order, lo, across=1)
    for chunk in range(chunks):
        pack[chunk, :rows, :] = cut[chunk * rows : chunk * rows + rows]

    stiff_in.wait()
    penalty_in.wait()
    eye = iota((64, 64), 0) == iota((64, 64), 1)
    lane64 = iota((64, 128), 1)
    diags = jnp.zeros((64, 128), f32)
    for s in range(24):
        if s < 8:
            p = prolong[s]
            kp = mm(stiff[...], p, highest)
            matrix = mm(p.T, kp, highest)
            templ[s] = matrix
        else:
            matrix = penalty[s - 8]
        column = jnp.sum(jnp.where(eye, matrix, 0.0), axis=1, keepdims=True)
        diags = jnp.where(lane64 == s, column, diags)
        hi, lo = split(matrix)
        two = jnp.concatenate([hi, lo], axis=1)
        for i in range(2):
            ops[i, s * 32 : s * 32 + 32, 0:128] = two[i * 32 : i * 32 + 32]
            ops[i, s * 32 : s * 32 + 32, 128:192] = hi[i * 32 : i * 32 + 32]

    pl.semaphore_wait(barrier, chunks - 1 + 2 + near - 1 + 1 + 1)

    def rho_copy(i, to_a, to_b):
        return pltpu.make_async_remote_copy(
            src_ref=rho,
            dst_ref=rho_in.at[i],
            send_sem=rho_ss.at[i],
            recv_sem=rho_rs.at[i],
            device_id=(to_a, to_b),
            device_id_type=MESH,
        )

    rho_copies = [
        rho_copy(DOWN_A, up_a, b),
        rho_copy(UP_A, down_a, b),
        rho_copy(DOWN_B, a, up_b),
        rho_copy(UP_B, a, down_b),
    ]
    for copy in rho_copies:
        copy.start()

    neigh_in.wait()
    codes_in.wait()
    for copy in rho_copies:
        copy.wait()
    lane, half = iota((rows, 128), 1), iota((rows, 128), 0) // q
    tile = jnp.ones((rows, 128), f32)
    face_w = []
    for m in range(2):
        for k in range(2):
            l = 2 * m + k
            own = rho[l : l + 1, :]
            faces = {
                DOWN_A: rho_in[DOWN_A, l : l + 1, :],
                UP_A: rho_in[UP_A, l : l + 1, :],
                DOWN_B: rho_in[DOWN_B, 2 + k : 3 + k, :] if m == 0 else rho[k : k + 1, :],
                UP_B: rho[2 + k : 3 + k, :] if m == 0 else rho_in[UP_B, k : k + 1, :],
                (UP_C if k == 0 else DOWN_C): rho[2 * m + 1 - k : 2 * m + 2 - k, :],
            }
            for c in range(8):
                at = (half == k) & (lane == m * 64 + slots[0, m, k, c])
                tile = jnp.where(at, dens[0, m, k, c], tile)
            face_w.append({})
            for face, other in faces.items():
                present = (neigh[0, m, k, face] >= 0).astype(f32)
                face_w[l][face] = 2.0 / (own + other) * present
    tile = 1.0 / tile
    for m in range(2):
        for k in range(2):
            for face in range(6):
                code = codes[0, m, k, face].astype(f32)
                weight = face_w[2 * m + k].get(face, jnp.zeros((1, 128), f32))
                tile = jnp.where((half == k) & (lane == m * 64 + 8 + face), code, tile)
                tile = jnp.where((half == k) & (lane == m * 64 + 14 + face), weight, tile)
    for chunk in range(chunks):
        pack[chunk, rows:, :] = tile

    def held_copy(d):
        chunk, where = device(d)
        return pltpu.make_async_remote_copy(
            src_ref=pack.at[chunk],
            dst_ref=held.at[core, a],
            send_sem=held_ss.at[d],
            recv_sem=held_rs.at[d],
            device_id=where,
            device_id_type=MESH,
        )

    for d in far_first:
        held_copy(d).start()
    held[core, a] = pack[mine]

    top = jnp.zeros((1, 1), f32)
    for m in range(2):
        for k in range(2):
            diag = jnp.zeros((64, 64), f32)
            for c in range(8):
                weight = 1.0 / jnp.full((1, 64), dens[0, m, k, c], f32)
                diag = diag + weight * templ[slots[0, m, k, c]]
            extent = jnp.zeros((64, 64), f32)
            for face, weight in face_w[2 * m + k].items():
                block = weight[:, :64] * penalty[codes[0, m, k, face]]
                diag = diag + block
                extent = extent + jnp.abs(block)
            jac = jnp.sum(jnp.where(eye, diag, 0.0), axis=1, keepdims=True)
            sums = jnp.sum(jnp.abs(diag) + extent, axis=1, keepdims=True)
            top = jnp.maximum(top, jnp.max(sums / jac, axis=0, keepdims=True))

    top_1[0] = jnp.broadcast_to(top, (8, 128))

    def top1_copy(d):
        return pltpu.make_async_remote_copy(
            src_ref=top_1.at[0],
            dst_ref=top_1.at[d],
            send_sem=top1_ss.at[d],
            recv_sem=top1_rs.at[d],
            device_id=device(d)[1],
            device_id_type=MESH,
        )

    def top2_copy(d):
        return pltpu.make_async_remote_copy(
            src_ref=top_2.at[0],
            dst_ref=top_2.at[d],
            send_sem=top2_ss.at[d],
            recv_sem=top2_rs.at[d],
            device_id=around(d),
            device_id_type=MESH,
        )

    each(1, chunks, lambda d: top1_copy(d).start())

    code16 = iota((16, 128), 0).astype(f32)

    def unpack(j, _):
        got = held[j - 2 * REACH]
        x = got[:, :rows, :].reshape(64, 128).T
        x = jnp.concatenate([x[:64], x[64:]], axis=1)
        meta = got[:, rows:, :].reshape(64, 128).T
        meta = jnp.concatenate([meta[0:32], meta[64:96]], axis=1)
        weights[j] = meta[0:24]
        summed = jnp.zeros((16, 128), f32)
        for face in range(6):
            summed = summed + jnp.where(
                code16 == meta[8 + face : 9 + face], meta[14 + face : 15 + face], 0.0
            )
        table = jnp.concatenate([meta[0:8], summed, jnp.zeros((104, 128), f32)], axis=0)
        over = 1.0 / mm(diags, table, highest)
        rhs[j] = x
        ijac[j] = over
        start[j] = x * over
        vec[j] = x * over
        return 0

    own_units = range(2 * REACH, 2 * REACH + 2)

    def products(t, which=None):
        def two(i, _):
            j = t // 2 + 2 * i
            hi, lo = split(jnp.concatenate([vec[j], vec[j + 1]], axis=1))
            stack = jnp.concatenate([hi, hi, lo], axis=0)
            for n in range(2):
                every = mm(ops[n], stack)
                at = slice(n * 32, n * 32 + 32)
                for u in range(2):
                    y = every[:, u * 128 : u * 128 + 128]
                    w = weights.at[j + u]

                    def flux_of(face):
                        code = jnp.broadcast_to(w[8 + face : 9 + face, :], (32, 128))
                        flux = y[256:288]
                        for c in range(1, 16):
                            flux = jnp.where(code == c, y[256 + c * 32 : 288 + c * 32], flux)
                        return w[14 + face : 15 + face, :] * flux

                    if j + u < (t + 1) // 2:
                        g_up[j + u, at, :] = flux_of(UP_B)
                        continue
                    if j + u >= UNITS - (t + 1) // 2:
                        g_down[j + u, at, :] = flux_of(DOWN_B)
                        continue
                    result = w[0:1, :] * y[0:32]
                    for s in range(1, 8):
                        result = result + w[s : s + 1, :] * y[s * 32 : s * 32 + 32]
                    g = []
                    for face in range(6):
                        g.append(flux_of(face))
                        result = result + g[face]
                    result = result - roll(g[UP_A], rows) - roll(g[DOWN_A], -rows)
                    part[j + u, at, :] = result - roll(g[UP_C], q) - roll(g[DOWN_C], -q)
                    g_up[j + u, at, :] = g[UP_B]
                    g_down[j + u, at, :] = g[DOWN_B]
            return 0

        for i in range(UNITS // 2 - t // 2) if which is None else which:
            two(i, 0)

    def applied(t, use):
        def one(j, _):
            below, above = max(j - 1, 0), min(j + 1, UNITS - 1)
            low = roll(jnp.where(left, g_up[j], g_up[below]), 64)
            high = roll(jnp.where(left, g_down[above], g_down[j]), 64)
            use(j, part[j] - low - high)
            return 0

        for j in range((t + 1) // 2, UNITS - (t + 1) // 2):
            one(j, 0)

    def keep_first(j, value):
        w0[j] = value
        vec[j] = value * ijac[j]

    each(1, chunks, lambda d: held_copy(d).wait())
    for j in range(2 * REACH, 2 * REACH + 2):
        unpack(j, 0)

    def base_copy(n, ref, side, d):
        return pltpu.make_async_remote_copy(
            src_ref=ref.at[2:4],
            dst_ref=ref.at[4 * side : 4 * side + 2],
            send_sem=base_ss.at[n, side],
            recv_sem=base_rs.at[n, side],
            device_id=along(d),
            device_id_type=MESH,
        )

    base_copies = [base_copy(0, base, 0, 1), base_copy(0, base, 1, pairs - 1)]
    more_copies = [base_copy(1, more, 0, 1), base_copy(1, more, 1, pairs - 1)]
    for copy in base_copies + more_copies:
        copy.start()
    products(0, (REACH,))
    each(1, chunks, lambda d: top1_copy(d).wait())
    top_2[0] = jnp.max(top_1[...], axis=0)
    each(1, near, lambda d: top2_copy(d).start())
    for copy in base_copies:
        copy.wait()
    for j in (0, 1, 4, 5):
        vec[j] = start[j]
    products(0, (0, 2 * REACH))
    for copy in more_copies:
        copy.wait()
    applied(0, keep_first)
    each(1, near, lambda d: top2_copy(d).wait())
    top_3[0] = jnp.max(top_2[...], axis=0)
    top3_copy = pltpu.make_async_remote_copy(
        src_ref=top_3.at[0],
        dst_ref=top_3.at[1],
        send_sem=top3_sems.at[0],
        recv_sem=top3_sems.at[1],
        device_id=opposite,
        device_id_type=MESH,
    )
    top3_copy.start()
    products(1)
    top3_copy.wait()
    upper = jnp.max(top_3[...], axis=0)[0:1, :]

    lower = upper / 10.0
    centre_val = 0.5 * (upper + lower)
    half_width = 0.5 * (upper - lower)
    sigma = centre_val / half_width
    over_centre = 1.0 / centre_val
    damp0 = 1.0 / sigma
    damp1 = 1.0 / (2.0 * sigma - damp0)
    keep1, gain1 = damp1 * damp0, 2.0 * damp1 / half_width
    damp2 = 1.0 / (2.0 * sigma - damp1)
    keep2, gain2 = damp2 * damp1, 2.0 * damp2 / half_width

    def combine(j, second):
        over, first = ijac[j], w0[j]
        update0 = rhs[j] * over * over_centre
        resid1 = rhs[j] - first * over_centre
        update1 = keep1 * update0 + gain1 * (resid1 * over)
        both = (keep1 * over_centre) * first + gain1 * (first - over_centre * second)
        resid2 = resid1 - both
        update2 = keep2 * update1 + gain2 * (resid2 * over)
        resid[j] = resid2
        if j in own_units:
            total[j - 2 * REACH] = update0 + update1 + update2
        vec[j] = update2

    applied(1, combine)

    def sweep(t, damp, multiply=products):
        damp_next = 1.0 / (2.0 * sigma - damp)
        keep, gain = damp_next * damp, 2.0 * damp_next / half_width

        def step(j, value):
            now = resid[j] - value
            resid[j] = now
            update = keep * vec[j] + gain * (now * ijac[j])
            if j in own_units:
                total[j - 2 * REACH] = total[j - 2 * REACH] + update
            vec[j] = update

        multiply(t)
        applied(t, step)
        return damp_next

    damp = damp2
    for t in range(2, SPAN):
        damp = sweep(t, damp)

    edge[0] = vec[2 * REACH : 2 * REACH + 2]
    edge[1] = resid[2 * REACH : 2 * REACH + 2]

    def edge_copy(n, side, d):
        return pltpu.make_async_remote_copy(
            src_ref=edge.at[n],
            dst_ref=edge_in.at[side, n],
            send_sem=edge_ss.at[n, side],
            recv_sem=edge_rs.at[n, side],
            device_id=along(d),
            device_id_type=MESH,
        )

    vec_copies, resid_copies = [
        [edge_copy(n, 0, 1), edge_copy(n, 1, pairs - 1)] for n in range(2)
    ]
    for copy in vec_copies + resid_copies:
        copy.start()
    products(0, (REACH,))
    for copy in vec_copies:
        copy.wait()
    for side in range(2):
        vec[4 * side : 4 * side + 2] = edge_in[side, 0]

    def outer(t):
        products(t, (0, 2 * REACH))
        for copy in resid_copies:
            copy.wait()
        for side in range(2):
            resid[4 * side : 4 * side + 2] = edge_in[side, 1]

    damp = sweep(0, damp, outer)
    for t in range(1, SWEEPS - SPAN):
        damp = sweep(t, damp)

    for u in range(2):
        x = total[u]
        done[u] = jnp.concatenate([x[:, :64], x[:, 64:]], axis=0).T

    def parts_copy(d):
        chunk, where = device(d)
        return pltpu.make_async_remote_copy(
            src_ref=done.at[lax.rem(chunk, 2)],
            dst_ref=parts.at[mine],
            send_sem=parts_ss.at[d],
            recv_sem=parts_rs.at[d],
            device_id=where,
            device_id_type=MESH,
        )

    for d in far_first:
        parts_copy(d).start()
    parts[mine] = done[core]
    each(1, chunks, lambda d: parts_copy(d).wait())

    even = lax.rem(iota((64, 128), 0), 2) == 0

    def out_copy(i):
        return pltpu.make_async_copy(ready.at[i], out.at[i], out_sems.at[i])

    def place(i, _):
        at = pl.ds(i * rows, rows)
        hi, lo = split(parts[:, at, :].reshape(128, 128).T)
        x = mm(hi, order) + mm(lo, order)
        for m in range(2):
            own = x[m * 64 : m * 64 + 64]
            turned = roll(own, 64)
            moved = jnp.where(even, pltpu.roll(turned, 63, 0), pltpu.roll(turned, 1, 0))
            ready[i, m] = jnp.where(even == left, own, moved)
        out_copy(i).start()
        return 0

    for i in range(slabs):
        place(i, 0)
    each(0, slabs, lambda i: out_copy(i).wait())


def local(slabs, grps, dens, slots, neigh, codes, stiff, prolong, penalty, fine):
    x = fine.reshape(4, 8, 32, 128).transpose(0, 2, 1, 3).reshape(4, 256, 128)
    smem, vmem = pltpu.SMEM, pltpu.VMEM
    args = (dens, slots, neigh, codes, stiff, prolong, penalty, x)
    dma = pltpu.SemaphoreType.DMA
    chunks, pairs = 2 * slabs, grps // 2
    rows = 128 // chunks
    columns = pltpu.VMEM((UNITS, 64, 128), f32)
    result = pl.pallas_call(
        functools.partial(kernel, slabs, grps),
        out_shape=jax.ShapeDtypeStruct((slabs, 2, 64, 128), f32),
        in_specs=[pl.BlockSpec(memory_space=pl.ANY)] * 8,
        out_specs=pl.BlockSpec(memory_space=pl.ANY),
        scratch_shapes=[
            *(space(v.shape, v.dtype) for space, v in zip([smem] * 4 + [vmem] * 4, args)),
            dma((8,)),
            pltpu.VMEM((8, 128), f32),
            pltpu.VMEM((4, 8, 128), f32),
            pltpu.VMEM((8, 64, 64), f32),
            pltpu.VMEM((256, 128), f32),
            pltpu.VMEM((2, 768, 192), bf16),
            pltpu.VMEM((chunks, 2 * rows, 128), f32),
            pltpu.VMEM((2, slabs, 2 * rows, 128), f32),
            pltpu.VMEM((UNITS, 88, 128), f32),
            pltpu.VMEM((UNITS, 128, 128), f32),
            *[columns] * 6,
            pltpu.VMEM((2, 64, 128), f32),
            pltpu.VMEM((chunks, 8, 128), f32),
            pltpu.VMEM((pairs // 2, 8, 128), f32),
            pltpu.VMEM((2, 8, 128), f32),
            pltpu.VMEM((2, 2, 64, 128), f32),
            pltpu.VMEM((2, 2, 2, 64, 128), f32),
            pltpu.VMEM((2, 64, 128), f32),
            pltpu.VMEM((chunks, 64, 128), f32),
            pltpu.VMEM((slabs, 2, 64, 128), f32),
            dma((slabs,)),
            dma((4,)),
            dma((4,)),
            dma((chunks,)),
            dma((chunks,)),
            dma((chunks,)),
            dma((chunks,)),
            dma((pairs // 2,)),
            dma((pairs // 2,)),
            dma((2,)),
            dma((2, 2)),
            dma((2, 2)),
            dma((2, 2)),
            dma((2, 2)),
            dma((chunks,)),
            dma((chunks,)),
        ],
        compiler_params=pltpu.CompilerParams(collective_id=0, has_side_effects=True),
    )(*args)
    spread = result.reshape(slabs, 2, 32, 2, 128).transpose(0, 1, 3, 2, 4)
    return spread.reshape(slabs, 2, 2, 4096)


def solution(mesh):
    return jax.shard_map(
        functools.partial(local, mesh.shape["slab"], mesh.shape["grp"]),
        mesh=mesh,
        in_specs=(
            P("slab", "grp", None, None),
            P("slab", "grp", None, None),
            P("slab", "grp", None, None),
            P("slab", "grp", None, None),
            P(),
            P(),
            P(),
            P("slab", "grp", None, None, None),
        ),
        out_specs=P(None, "grp", None, None),
        check_vma=False,
    )
```
